32 devices in a mesh: shots: 2 (over x), gx: 16 (over z, y, core).
Axes of the slice: x: 2, y: 2, z: 4, core: 2. Of those that a mesh axis runs over, the one named last changes fastest.
Arguments:
- courant_sq: float32 [128, 128, 128], P('gx'), may hold values from 0.03 to 0.2
- wave_prev: float32 [256, 128, 128], P(('shots', 'gx')), parts along dimension 0, may hold values from -6 to 6
- wave_now: float32 [256, 128, 128], P(('shots', 'gx')), parts along dimension 0, may hold values from -6 to 6
- adj_late: float32 [256, 128, 128], P(('shots', 'gx')), parts along dimension 0, may hold values from -6 to 6
- adj_last: float32 [256, 128, 128], P(('shots', 'gx')), parts along dimension 0, may hold values from -6 to 6
- wavelet: float32 [24], P('shots'), parts along dimension 0, may hold values from -48 to 48
- source_cell: int32 [2], P('shots'), parts along dimension 0, may hold values from 0 to 2097151
- receivers: int32 [2048], P('shots'), parts along dimension 0, may hold values from 0 to 2097151
- observed: float32 [24, 1024], P('shots'), parts along dimension 0, may hold values from -6 to 6
- footprint: int32 [4096], P(('shots', 'gx')), parts along dimension 0, may hold values 0 or 1
- brick_owner: int32 [2048, 1], P('gx'), may hold values from 0 to 15; in each aligned block of 128 rows (0 to 127, 128 to 255, ...) at most 16 rows name the same one
- prior_in: bfloat16 [32, 27], replicated, may hold values from -1.25 to 1.25
- prior_in_bias: float32 [32], replicated, may hold values from -3 to 3
- prior_mix: bfloat16 [32, 32], replicated, may hold values from -1 to 1
- prior_mix_bias: float32 [32], replicated, may hold values from -3 to 3
- prior_out: bfloat16 [27, 32], replicated, may hold values from -0.21875 to 0.21875
- prior_out_bias: float32 [1], replicated, may hold values from -3 to 3
Outputs:
- residual_traces: float32 [24, 1024], P('shots'), parts along dimension 0
- owned_bricks: bfloat16 [32, 16, 16, 1024], P(('shots', 'gx')), parts along dimension 0
The draws below stay inside these ranges and needn't reach their ends.
There are 2 independent parts, one for each index of `shots`. The reference program is written for one: setup_inputs(seed, part) draws one part's arguments, and reference() takes and returns one part's arrays. A program takes and returns all parts, laid end to end along the dimension named above; an argument that names none is the same for every part. Nothing has to cross between parts.
Inputs may be any that keep to these rules, and one draw needn't show every extreme that they name: `brick_owner`: among the 128 bricks of one device's block, at most 16 have the same owner.
All inputs are finite; a program needn't handle non-finite values. No bound on the sum of `footprint` on one device may be relied on, other than what follows from the above.
Results may differ from the reference program's by a relative error of at most 0.0045.
Values may be sent and summed in bfloat16 or wider, within the bound.
A program may use at most 128 MiB of HBM per device.

```python
import math
import jax
import jax.numpy as jnp
import numpy as np
from jax import lax

CX = 8
NY = 128
NZ = 128
STEPS = 12
NREC = 1024
CH = 32
NX = 128
SOURCES = 16
BRICKS = 2048
CAP = 16
N_GX = 16


def touch_ends(array, stream_key, low, top_value):
    extent = array.shape
    index_at = [jax.random.randint(jax.random.fold_in(stream_key, axis), (), 0, extent[axis]) for axis in range(len(extent))]
    array = array.at[tuple(index_at)].set(low)
    longest = extent.index(max(extent))
    index_at[longest] = (index_at[longest] + 1) % extent[longest]
    return array.at[tuple(index_at)].set(top_value)


def level_of(stream_key, shape, shards, smallest, largest):
    loudness = 1.0
    for dim, parts in shards:
        heights = jax.random.uniform(jax.random.fold_in(jax.random.fold_in(stream_key, 6), dim), (parts,), jnp.float32, smallest / len(shards), largest / len(shards))
        loudness = loudness * jnp.repeat(jnp.exp(heights), shape[dim] // parts).reshape((-1,) + (1,) * (len(shape) - 1 - dim))
    return loudness


def shared_out(rng, own, number, rows, amount, top, limit, lean):
    order = jax.random.permutation(rng, amount)
    heavy_load, common = shares(amount, rows * top, limit, lean, True), shares(amount, rows * top, limit, lean, False)
    places = jnp.arange(amount)

    def named(sizes, turn):
        used = int((sizes > 0).sum())
        fixed = max(1, used // 4)
        shifted = fixed + (places - fixed + turn * (used - fixed)) % max(1, amount - fixed)
        return jnp.zeros((amount,), jnp.int32).at[order[jnp.where(places < fixed, places, shifted)]].set(jnp.asarray(sizes, jnp.int32))

    sizes = jnp.where(number % 4 == 0, named(heavy_load, number // 4), named(common, number - number // 4 - 1))
    mixed = jax.random.permutation(jax.random.fold_in(own, 3), amount)
    donor, receiver = mixed[0:amount // 2 * 2:2], mixed[1:amount // 2 * 2:2]
    margin = jnp.minimum(sizes[donor] - 1, limit - sizes[receiver]) // 2
    margin = jnp.where((donor == order[0]) | (receiver == order[0]) | (sizes[receiver] == 0), 0, jnp.maximum(margin, 0))
    shifted = jax.random.randint(jax.random.fold_in(own, 4), (amount // 2,), 0, 1 << 20) % (margin + 1)
    sizes = sizes.at[donor].add(-shifted).at[receiver].add(shifted)
    labels = jnp.searchsorted(jnp.cumsum(sizes), jnp.arange(rows * top), side="right").astype(jnp.int32)
    grid = labels.reshape(top, rows).T
    grid = grid[jax.random.permutation(jax.random.fold_in(own, 1), rows)]
    turn = jax.random.randint(jax.random.fold_in(own, 2), (rows, 1), 0, top)
    return jnp.take_along_axis(grid, (jnp.arange(top)[None, :] + turn) % top, axis=1)


def shares(count, total, bound, lean, full):
    portions = [(1 << 20) // math.isqrt(grade ** lean) + 1 for grade in range(1, count + 1)]
    largest = bound if full else min(bound, max(-(-total // count), total * portions[0] // sum(portions)))
    least = 1 if total - largest >= count - 1 else 0
    holding, rest = [largest] + [least] * (count - 1), total - largest - least * (count - 1)
    while rest > 0:
        movable = [i for i in range(1, count) if holding[i] < largest] or [i for i in range(1, count) if holding[i] < bound]
        mass, remaining = sum([portions[i] for i in movable]), rest
        for i in movable:
            extra = min(bound - holding[i], max(1, remaining * portions[i] // mass), rest)
            holding[i] = holding[i] + extra
            rest = rest - extra
    return np.array(holding)


def normal_values(rng, dims, deviation, most, shards=(), held_as=jnp.bfloat16):
    result = jax.random.normal(rng, dims, jnp.float32) * deviation
    if len(shards) > 0:
        result = level_of(rng, dims, shards, -0.22, 0.18) * result
    return jnp.clip(result, min=-most, max=most).astype(held_as)


def setup_inputs(seed: int = 0, part: int = 0) -> dict:
    key_list = jax.random.split(jax.random.key(seed), 18)
    own_keys = jax.random.split(jax.random.fold_in(key_list[17], part), 18)
    courant_sq = jnp.clip(jnp.exp(math.log(0.2) - 1.89712 * jax.random.uniform(key_list[0], (NX, NY, NZ), jnp.float32) ** level_of(key_list[0], (NX, NY, NZ), ((0, 16),), -0.2, 0.2)), 0.03, 0.2)
    wave_prev = normal_values(own_keys[1], (NX, NY, NZ), 1.0, 6.0, ((0, 16),), jnp.float32)
    wave_now = normal_values(own_keys[2], (NX, NY, NZ), 1.0, 6.0, ((0, 16),), jnp.float32)
    adj_late = normal_values(own_keys[3], (NX, NY, NZ), 1.0, 6.0, ((0, 16),), jnp.float32)
    adj_last = normal_values(own_keys[4], (NX, NY, NZ), 1.0, 6.0, ((0, 16),), jnp.float32)
    wavelet = normal_values(own_keys[5], (STEPS,), 8.0, 48.0, (), jnp.float32)
    source_cell = jax.random.randint(own_keys[6], (1,), 0, NX * NY * NZ).astype(jnp.int32)
    receivers = touch_ends(jax.random.randint(own_keys[7], (NREC,), 0, NX * NY * NZ), jax.random.fold_in(own_keys[7], 1), 0, (NX * NY * NZ) - 1).astype(jnp.int32)
    observed = normal_values(own_keys[8], (STEPS, NREC), 1.0, 6.0, (), jnp.float32)
    footprint = touch_ends((jax.random.randint(own_keys[9], (BRICKS,), 0, 4) < 3).astype(jnp.int32), jax.random.fold_in(own_keys[9], 1), 0, 1)
    brick_owner_keys = jax.random.split(jax.random.fold_in(key_list[10], 1), BRICKS // NY)
    brick_owner_turns = jax.random.permutation(jax.random.fold_in(key_list[10], 3), BRICKS // NY)
    brick_owner = jax.vmap(lambda own, number: shared_out(jax.random.fold_in(key_list[10], 2), own, number, NY, SOURCES, 1, CAP, 2))(brick_owner_keys, brick_owner_turns).reshape((BRICKS, 1))
    prior_in = normal_values(key_list[11], (CH, 27), 27 ** -0.5, 1.25)
    prior_in_bias = normal_values(key_list[12], (CH,), 0.5, 3.0, (), jnp.float32)
    prior_mix = normal_values(key_list[13], (CH, CH), CH ** -0.5, 1.0)
    prior_mix_bias = normal_values(key_list[14], (CH,), 0.5, 3.0, (), jnp.float32)
    prior_out = normal_values(key_list[15], (27, CH), (27 * CH) ** -0.5, 0.21875)
    prior_out_bias = normal_values(key_list[16], (1,), 0.5, 3.0, (), jnp.float32)
    return dict(courant_sq=courant_sq, wave_prev=wave_prev, wave_now=wave_now, adj_late=adj_late, adj_last=adj_last, wavelet=wavelet, source_cell=source_cell, receivers=receivers, observed=observed, footprint=footprint, brick_owner=brick_owner, prior_in=prior_in, prior_in_bias=prior_in_bias, prior_mix=prior_mix, prior_mix_bias=prior_mix_bias, prior_out=prior_out, prior_out_bias=prior_out_bias)


OFFSETS = [(a, b, c) for a in range(3) for b in range(3) for c in range(3)]


def laplace(widened):
    inner = widened[2:-2]
    along_x = 16.0 * (widened[3:-1] + widened[1:-3]) - (widened[4:] + widened[:-4])
    pad_y = jnp.pad(inner, ((0, 0), (2, 2), (0, 0)))
    along_y = 16.0 * (pad_y[:, 3:-1] + pad_y[:, 1:-3]) - (pad_y[:, 4:] + pad_y[:, :-4])
    pad_z = jnp.pad(inner, ((0, 0), (0, 0), (2, 2)))
    along_z = 16.0 * (pad_z[:, :, 3:-1] + pad_z[:, :, 1:-3]) - (pad_z[:, :, 4:] + pad_z[:, :, :-4])
    return (along_x + along_y + along_z - 90.0 * inner) / 12.0


def leapfrog(before, widened, coeffs):
    return 2.0 * widened[2:-2] - before + coeffs * laplace(widened)


def inject(field, base_x, cells, values):
    plane = field.shape[1] * field.shape[2]
    count = field.shape[0] * plane
    relative = cells - base_x * plane
    inside = (relative >= 0) & (relative < count)
    clipped = jnp.clip(relative, 0, count - 1)
    flattened = field.reshape(-1).at[clipped].add(jnp.where(inside, values, 0.0))
    return flattened.reshape(field.shape)


def sample(field, base_x, cells):
    plane = field.shape[1] * field.shape[2]
    count = field.shape[0] * plane
    relative = cells - base_x * plane
    inside = (relative >= 0) & (relative < count)
    clipped = jnp.clip(relative, 0, count - 1)
    return jnp.where(inside, field.reshape(-1)[clipped], 0.0)


def lifting(widened, weight_in, bias_in, weight_mix, bias_mix):
    planes = widened.shape[0] - 2
    rows_y = widened.shape[1]
    rows_z = widened.shape[2]
    padded = jnp.pad(widened, ((0, 0), (1, 1), (1, 1)))
    stacked = jnp.stack([padded[a:a + planes, b:b + rows_y, c:c + rows_z] for a, b, c in OFFSETS]).reshape(27, -1)
    lifted = jnp.dot(weight_in, stacked, preferred_element_type=jnp.float32) + bias_in[:, None]
    lifted = jnp.maximum(lifted, 0.0).astype(jnp.bfloat16)
    hidden = jnp.dot(weight_mix, lifted, preferred_element_type=jnp.float32) + bias_mix[:, None]
    return jnp.maximum(hidden, 0.0).astype(jnp.bfloat16).reshape(-1, planes, rows_y, rows_z)


def project(widened, weight_out, bias_out):
    channels = widened.shape[0]
    planes = widened.shape[1] - 2
    rows_y = widened.shape[2]
    rows_z = widened.shape[3]
    products = jnp.dot(weight_out, widened.reshape(channels, -1), preferred_element_type=jnp.float32)
    products = jnp.pad(products.reshape(27, planes + 2, rows_y, rows_z), ((0, 0), (0, 0), (1, 1), (1, 1)))
    summed = jnp.zeros((planes, rows_y, rows_z), jnp.float32)
    for position, (a, b, c) in enumerate(OFFSETS):
        summed = summed + products[position, a:a + planes, b:b + rows_y, c:c + rows_z]
    return summed + bias_out[0]


def reference(courant_sq, wave_prev, wave_now, adj_late, adj_last, wavelet, source_cell, receivers, observed, footprint, brick_owner, prior_in, prior_in_bias, prior_mix, prior_mix_bias, prior_out, prior_out_bias):
    def widen(field):
        return jnp.pad(field, ((2, 2), (0, 0), (0, 0)))

    before, current = wave_prev, wave_now
    changes = []
    records = []
    for t in range(STEPS):
        newest = inject(leapfrog(before, widen(current), courant_sq), 0, source_cell, wavelet[t:t + 1])
        records.append(sample(newest, 0, receivers))
        changes.append(newest - 2.0 * current + before)
        before, current = current, newest
    residual_traces = jnp.stack(records) - observed
    future, current = adj_late, adj_last
    grad = jnp.zeros(wave_now.shape, jnp.float32)
    for t in range(STEPS - 1, -1, -1):
        newest = inject(leapfrog(future, widen(current), courant_sq), 0, receivers, residual_traces[t])
        grad = grad + newest * changes[t]
        future, current = current, newest
    grad_low = grad.astype(jnp.bfloat16)
    padded = jnp.pad(grad_low, ((2, 2), (0, 0), (0, 0)))

    def block_fn(block):
        start = (block * CX).astype(jnp.int32)
        piece = lax.dynamic_slice_in_dim(padded, start, CX + 4, 0)
        hidden = lifting(piece, prior_in, prior_in_bias, prior_mix, prior_mix_bias)
        coords = start - 1 + jnp.arange(CX + 2, dtype=jnp.int32)
        keep = ((coords >= 0) & (coords < NX))[None, :, None, None]
        hidden = jnp.where(keep, hidden, jnp.zeros_like(hidden))
        return project(hidden, prior_out, prior_out_bias)

    conv = lax.map(block_fn, jnp.arange(NX // CX, dtype=jnp.int32)).reshape(NX, NY, NZ)
    model_grad = (grad + conv).astype(jnp.bfloat16)
    bricks = model_grad.reshape(N_GX, CX, NY, NZ).transpose(0, 2, 1, 3).reshape(N_GX * NY, CX * NZ)
    bricks = jnp.where((footprint == 1)[:, None], bricks, jnp.zeros_like(bricks))
    owners = brick_owner[:, 0].reshape(N_GX, NY)
    same = owners[:, :, None] == owners[:, None, :]
    lower = jnp.arange(NY, dtype=jnp.int32)[:, None] > jnp.arange(NY, dtype=jnp.int32)[None, :]
    slots = jnp.sum((same & lower[None]).astype(jnp.int32), axis=2)
    sources = jnp.repeat(jnp.arange(N_GX, dtype=jnp.int32), NY)
    owned = jnp.zeros((N_GX, N_GX, CAP, CX * NZ), jnp.bfloat16)
    owned = owned.at[owners.reshape(-1), sources, slots.reshape(-1)].set(bricks)
    return residual_traces, owned
```

```python
import functools
import jax
import jax.numpy as jnp
from jax import lax
from jax.experimental import pallas as pl
from jax.experimental.pallas import tpu as pltpu
from jax.sharding import PartitionSpec as P

OFFSETS = [(a, b, c) for a in range(3) for b in range(3) for c in range(3)]


MESH = pl.DeviceIdType.MESH
PAD = 8


def wave_kernel(
    n,
    c_ref,
    wave_prev,
    wave_now,
    adj_late,
    adj_last,
    wavelet,
    source,
    row_lane,
    z_lane,
    row_sub,
    z_sub,
    observed,
    grad_ref,
    wide_ref,
    resid_ref,
    fwd,
    adj,
    changes,
    c12,
    src,
    inj,
    hot,
    hot_t,
    zhot,
    zhot_t,
    parts,
    inj_parts,
    rec_send,
    rec_recv,
    resid8,
    f_send,
    f_recv,
    a_send,
    a_recv,
    r_send,
    r_recv,
    g_send,
    g_recv,
):
    cx, ny, nz = c_ref.shape
    steps = changes.shape[0]
    nrec = row_lane.shape[1]
    groups = nrec // 128
    rows = cx * ny
    me = lax.axis_index("gx")
    shot = lax.axis_index("shots")

    barrier = pltpu.get_barrier_semaphore()

    for buf in (fwd, adj):
        for k in range(3):
            buf[k] = jnp.zeros(buf.shape[1:], jnp.float32)
    wide_ref[0:2] = jnp.zeros((2, ny, nz), jnp.bfloat16)
    wide_ref[cx + 2 : cx + 4] = jnp.zeros((2, ny, nz), jnp.bfloat16)
    def greet(d, carry):
        pl.semaphore_signal(
            barrier, inc=1, device_id=(shot, lax.rem(me + d, n)), device_id_type=MESH
        )
        return carry

    lax.fori_loop(1, n, greet, 0)

    inner = pl.ds(PAD, ny)
    for i in range(cx):
        fwd[0, i + 2, inner] = wave_prev[i]
        fwd[1, i + 2, inner] = wave_now[i]
        adj[0, i + 2, inner] = adj_late[i]
        adj[1, i + 2, inner] = adj_last[i]
    pl.semaphore_wait(barrier, n - 1)

    def halo(buf, k, send, recv, up):
        lo = cx if up else 2
        to = 0 if up else cx + 2
        side = 1 if up else 0
        return pltpu.make_async_remote_copy(
            src_ref=buf.at[k, pl.ds(lo, 2), inner],
            dst_ref=buf.at[k, pl.ds(to, 2), inner],
            send_sem=send.at[side],
            recv_sem=recv.at[k, side],
            device_id=(shot, me + 1 if up else me - 1),
            device_id_type=MESH,
        )

    def start_side(buf, k, send, recv, up):
        @pl.when((me < n - 1) if up else (me > 0))
        def _():
            halo(buf, k, send, recv, up).start()

    def wait_side(buf, k, send, recv):
        @pl.when(me < n - 1)
        def _():
            halo(buf, k, send, recv, True).wait_send()
            halo(buf, k, send, recv, False).wait_recv()

        @pl.when(me > 0)
        def _():
            halo(buf, k, send, recv, False).wait_send()
            halo(buf, k, send, recv, True).wait_recv()

    for up in (False, True):
        start_side(fwd, 1, f_send, f_recv, up)
    for up in (False, True):
        start_side(adj, 1, a_send, a_recv, up)

    for i in range(cx):
        c12[i] = c_ref[i] * (1.0 / 12.0)
    y_at = lax.broadcasted_iota(jnp.int32, (ny, nz), 0)
    z_at = lax.broadcasted_iota(jnp.int32, (ny, nz), 1)
    for i in range(cx):
        flat = ((me * cx + i) * ny + y_at) * nz + z_at
        src[i] = jnp.where(flat == source[0], 1.0, 0.0)

    def build(j, carry):
        at = pl.ds(pl.multiple_of(j * 128, 128), 128)
        r_iota = lax.broadcasted_iota(jnp.int32, (128, nrec), 0) + j * 128
        hot[at, :] = jnp.where(r_iota == row_lane[...], 1.0, 0.0).astype(jnp.bfloat16)
        return carry

    lax.fori_loop(0, rows // 128, build, 0)

    def build_t(j, carry):
        at = pl.ds(pl.multiple_of(j * 128, 128), 128)
        r_iota = lax.broadcasted_iota(jnp.int32, (128, rows), 1)
        hot_t[at, :] = jnp.where(r_iota == row_sub[at, :], 1.0, 0.0).astype(jnp.bfloat16)
        lane = lax.broadcasted_iota(jnp.int32, (128, nz), 1)
        zhot[at, :] = jnp.where(lane == z_sub[at, :], 1.0, 0.0)
        return carry

    lax.fori_loop(0, groups, build_t, 0)
    zhot_t[...] = jnp.where(
        lax.broadcasted_iota(jnp.int32, (nz, nrec), 0) == z_lane[...], 1.0, 0.0
    )

    chunk = 32
    lane = lax.broadcasted_iota(jnp.int32, (chunk, nz), 1)

    def laplace12(buf, k, i, y):
        def at(plane, dy):
            return buf[k, plane, pl.ds(PAD + y + dy, chunk), :]

        mid = at(i + 2, 0)
        near = (at(i + 3, 0) + at(i + 1, 0)) + (at(i + 2, 1) + at(i + 2, -1))
        far = (at(i + 4, 0) + at(i, 0)) + (at(i + 2, 2) + at(i + 2, -2))
        near += jnp.where(lane >= 1, pltpu.roll(mid, 1, 1), 0.0)
        near += jnp.where(lane < nz - 1, pltpu.roll(mid, nz - 1, 1), 0.0)
        far += jnp.where(lane >= 2, pltpu.roll(mid, 2, 1), 0.0)
        far += jnp.where(lane < nz - 2, pltpu.roll(mid, nz - 2, 1), 0.0)
        return mid, 16.0 * near - far - 90.0 * mid

    order = [0, 1, cx - 2, cx - 1] + list(range(2, cx - 2))

    def send_records(t):
        def one(d, carry):
            pltpu.make_async_remote_copy(
                src_ref=rec_send.at[t],
                dst_ref=rec_recv.at[t, d - 1],
                send_sem=r_send.at[t],
                recv_sem=r_recv.at[t],
                device_id=(shot, lax.rem(me + d, n)),
                device_id_type=MESH,
            ).start()
            return carry

        lax.fori_loop(1, n, one, 0)

    def forward(t, carry):
        prev, cur, nxt = lax.rem(t, 3), lax.rem(t + 1, 3), lax.rem(t + 2, 3)
        impulse = wavelet[t]
        wait_side(fwd, cur, f_send, f_recv)
        for done, i in enumerate(order):
            for y in range(0, ny, chunk):
                mid, lap = laplace12(fwd, cur, i, y)
                at = pl.ds(y, chunk)
                change = c12[i, at] * lap + impulse * src[i, at]
                changes[t, i, at] = change
                newest = 2.0 * mid - fwd[prev, i + 2, pl.ds(PAD + y, chunk)] + change
                fwd[nxt, i + 2, pl.ds(PAD + y, chunk)] = newest
                high = newest.astype(jnp.bfloat16)
                parts[pl.ds(i * ny + y, chunk), 0:nz] = high
                parts[pl.ds(i * ny + y, chunk), nz : 2 * nz] = (
                    newest - high.astype(jnp.float32)
                ).astype(jnp.bfloat16)
            if done == 1:

                @pl.when(t < steps - 1)
                def _():
                    start_side(fwd, nxt, f_send, f_recv, False)

            if done == 3:

                @pl.when(t < steps - 1)
                def _():
                    start_side(fwd, nxt, f_send, f_recv, True)

        picked = jnp.dot(hot_t[...], parts[...], preferred_element_type=jnp.float32)
        zsel = zhot[...]
        ones = jnp.ones((8, nz), jnp.bfloat16)
        total = jnp.zeros((8, nrec), jnp.float32)
        for h in range(2):
            kept = (picked[:, h * nz : (h + 1) * nz] * zsel).astype(jnp.bfloat16)
            total += lax.dot_general(
                ones, kept, (((1,), (1,)), ((), ())), preferred_element_type=jnp.float32
            )
        for g in range(groups):
            rec_send[t, g : g + 1, :] = total[0:1, g * 128 : (g + 1) * 128]
        send_records(t)
        return carry

    lax.fori_loop(0, steps, forward, 0)

    for i in range(cx):
        grad_ref[i] = jnp.zeros((ny, nz), jnp.float32)

    def backward(s, carry):
        t = steps - 1 - s
        prev, cur, nxt = lax.rem(s, 3), lax.rem(s + 1, 3), lax.rem(s + 2, 3)
        arrived = rec_recv.at[t]
        pltpu.make_async_copy(arrived, arrived, r_recv.at[t]).wait()
        pltpu.make_async_copy(arrived, arrived, r_send.at[t]).wait()
        total = rec_send[t] + jnp.sum(rec_recv[t], axis=0)
        misfit = total - observed[t]
        resid_ref[t] = misfit
        resid8[...] = misfit
        for g in range(groups):
            at = pl.ds(g * 128, 128)
            value = zhot_t[:, at] * resid8[g : g + 1, :]
            high = value.astype(jnp.bfloat16)
            inj_parts[pl.ds(0, nz), at] = high
            inj_parts[pl.ds(nz, nz), at] = (value - high.astype(jnp.float32)).astype(jnp.bfloat16)
        spread = lax.dot_general(
            hot[...], inj_parts[...], (((1,), (1,)), ((), ())), preferred_element_type=jnp.float32
        )
        inj[...] = spread[:, 0:nz] + spread[:, nz : 2 * nz]
        wait_side(adj, cur, a_send, a_recv)
        for done, i in enumerate(order):
            for y in range(0, ny, chunk):
                mid, lap = laplace12(adj, cur, i, y)
                at = pl.ds(y, chunk)
                newest = (
                    2.0 * mid
                    - adj[prev, i + 2, pl.ds(PAD + y, chunk)]
                    + (c12[i, at] * lap + inj[pl.ds(i * ny + y, chunk), :])
                )
                adj[nxt, i + 2, pl.ds(PAD + y, chunk)] = newest
                grad_ref[i, at] = grad_ref[i, at] + newest * changes[t, i, at]
            if done == 1:

                @pl.when(s < steps - 1)
                def _():
                    start_side(adj, nxt, a_send, a_recv, False)

            if done == 3:

                @pl.when(s < steps - 1)
                def _():
                    start_side(adj, nxt, a_send, a_recv, True)

        return carry

    lax.fori_loop(0, steps, backward, 0)

    for i in range(cx):
        wide_ref[i + 2] = grad_ref[i].astype(jnp.bfloat16)

    def edge(up):
        side = 1 if up else 0
        return pltpu.make_async_remote_copy(
            src_ref=wide_ref.at[pl.ds(cx if up else 2, 2)],
            dst_ref=wide_ref.at[pl.ds(0 if up else cx + 2, 2)],
            send_sem=g_send.at[side],
            recv_sem=g_recv.at[side],
            device_id=(shot, me + 1 if up else me - 1),
            device_id_type=MESH,
        )

    @pl.when(me < n - 1)
    def _():
        edge(True).start()

    @pl.when(me > 0)
    def _():
        edge(False).start()

    @pl.when(me < n - 1)
    def _():
        edge(True).wait_send()
        edge(False).wait_recv()

    @pl.when(me > 0)
    def _():
        edge(False).wait_send()
        edge(True).wait_recv()


def wave(n, c, wave_prev, wave_now, adj_late, adj_last, wavelet, source, receivers, observed):
    cx, ny, nz = c.shape
    steps, nrec = observed.shape
    rows = cx * ny
    relative = receivers - lax.axis_index("gx") * (rows * nz)
    inside = (relative >= 0) & (relative < rows * nz)
    row = jnp.where(inside, relative // nz, -1)
    z = jnp.where(inside, relative % nz, -1)
    vmem = pl.BlockSpec(memory_space=pltpu.VMEM)
    smem = pl.BlockSpec(memory_space=pltpu.SMEM)
    groups = nrec // 128
    f32, bf16 = jnp.float32, jnp.bfloat16
    grad, wide, resid = pl.pallas_call(
        functools.partial(wave_kernel, n),
        out_shape=(
            jax.ShapeDtypeStruct((cx, ny, nz), f32),
            jax.ShapeDtypeStruct((cx + 4, ny, nz), bf16),
            jax.ShapeDtypeStruct((steps, groups, 128), f32),
        ),
        in_specs=[vmem] * 5 + [smem] * 2 + [vmem] * 5,
        out_specs=(vmem, vmem, vmem),
        scratch_shapes=[
            pltpu.VMEM((3, cx + 4, ny + 2 * PAD, nz), f32),
            pltpu.VMEM((3, cx + 4, ny + 2 * PAD, nz), f32),
            pltpu.VMEM((steps, cx, ny, nz), f32),
            pltpu.VMEM((cx, ny, nz), f32),
            pltpu.VMEM((cx, ny, nz), f32),
            pltpu.VMEM((rows, nz), f32),
            pltpu.VMEM((rows, nrec), bf16),
            pltpu.VMEM((nrec, rows), bf16),
            pltpu.VMEM((nrec, nz), f32),
            pltpu.VMEM((nz, nrec), f32),
            pltpu.VMEM((rows, 2 * nz), bf16),
            pltpu.VMEM((2 * nz, nrec), bf16),
            pltpu.VMEM((steps, groups, 128), f32),
            pltpu.VMEM((steps, n - 1, groups, 128), f32),
            pltpu.VMEM((groups, 128), f32),
            pltpu.SemaphoreType.DMA((2,)),
            pltpu.SemaphoreType.DMA((3, 2)),
            pltpu.SemaphoreType.DMA((2,)),
            pltpu.SemaphoreType.DMA((3, 2)),
            pltpu.SemaphoreType.DMA((steps,)),
            pltpu.SemaphoreType.DMA((steps,)),
            pltpu.SemaphoreType.DMA((2,)),
            pltpu.SemaphoreType.DMA((2,)),
        ],
        compiler_params=pltpu.CompilerParams(
            collective_id=0, has_side_effects=True, vmem_limit_bytes=56 * 2**20
        ),
        name="wave",
    )(
        c,
        wave_prev,
        wave_now,
        adj_late,
        adj_last,
        wavelet,
        source,
        row[None, :],
        z[None, :],
        row[:, None],
        z[:, None],
        observed.reshape(steps, groups, 128),
    )
    return grad, wide, resid.reshape(steps, nrec)


def lifting(widened, weight_in, bias_in, weight_mix, bias_mix):
    planes = widened.shape[0] - 2
    rows_y = widened.shape[1]
    rows_z = widened.shape[2]
    padded = jnp.pad(widened, ((0, 0), (1, 1), (1, 1)))
    stacked = jnp.stack(
        [padded[a : a + planes, b : b + rows_y, c : c + rows_z] for a, b, c in OFFSETS]
    ).reshape(27, -1)
    lifted = jnp.dot(weight_in, stacked, preferred_element_type=jnp.float32) + bias_in[:, None]
    lifted = jnp.maximum(lifted, 0.0).astype(jnp.bfloat16)
    hidden = jnp.dot(weight_mix, lifted, preferred_element_type=jnp.float32) + bias_mix[:, None]
    return jnp.maximum(hidden, 0.0).astype(jnp.bfloat16).reshape(-1, planes, rows_y, rows_z)


def project(widened, weight_out, bias_out):
    channels = widened.shape[0]
    planes = widened.shape[1] - 2
    rows_y = widened.shape[2]
    rows_z = widened.shape[3]
    products = jnp.dot(
        weight_out, widened.reshape(channels, -1), preferred_element_type=jnp.float32
    )
    products = jnp.pad(
        products.reshape(27, planes + 2, rows_y, rows_z), ((0, 0), (0, 0), (1, 1), (1, 1))
    )
    summed = jnp.zeros((planes, rows_y, rows_z), jnp.float32)
    for position, (a, b, c) in enumerate(OFFSETS):
        summed = summed + products[position, a : a + planes, b : b + rows_y, c : c + rows_z]
    return summed + bias_out[0]


def per_device(
    courant_sq,
    wave_prev,
    wave_now,
    adj_late,
    adj_last,
    wavelet,
    source_cell,
    receivers,
    observed,
    footprint,
    brick_owner,
    prior_in,
    prior_in_bias,
    prior_mix,
    prior_mix_bias,
    prior_out,
    prior_out_bias,
):
    cells_x, cells_y, cells_z = wave_now.shape
    devices = lax.axis_size("gx")
    anchor = lax.axis_index("gx") * cells_x
    total_x = cells_x * devices
    grad, grad_wide, residual_traces = wave(
        devices,
        courant_sq,
        wave_prev,
        wave_now,
        adj_late,
        adj_last,
        wavelet,
        source_cell,
        receivers,
        observed,
    )
    hidden = lifting(grad_wide, prior_in, prior_in_bias, prior_mix, prior_mix_bias)
    margin = anchor - 1 + jnp.arange(cells_x + 2, dtype=jnp.int32)
    keep = ((margin >= 0) & (margin < total_x))[None, :, None, None]
    hidden_wide = jnp.where(keep, hidden, jnp.zeros_like(hidden))
    conv = project(hidden_wide, prior_out, prior_out_bias)
    model_grad = (grad + conv).astype(jnp.bfloat16)
    bricks = model_grad.transpose(1, 0, 2).reshape(cells_y, cells_x * cells_z)
    bricks = jnp.where((footprint == 1)[:, None], bricks, jnp.zeros_like(bricks))
    owners = brick_owner[:, 0]
    same = owners[:, None] == owners[None, :]
    lower = (
        jnp.arange(cells_y, dtype=jnp.int32)[:, None]
        > jnp.arange(cells_y, dtype=jnp.int32)[None, :]
    )
    slots = jnp.sum((same & lower).astype(jnp.int32), axis=1)
    capacity = max(2, 2 * cells_y // devices)
    buckets = (
        jnp.zeros((devices, capacity, cells_x * cells_z), jnp.bfloat16)
        .at[owners, slots]
        .set(bricks)
    )
    arrived = lax.all_to_all(buckets, "gx", split_axis=0, concat_axis=0, tiled=True)
    return (residual_traces, arrived[None])


def solution(mesh):
    return jax.shard_map(
        per_device,
        mesh=mesh,
        in_specs=(
            P("gx", None, None),
            P(("shots", "gx"), None, None),
            P(("shots", "gx"), None, None),
            P(("shots", "gx"), None, None),
            P(("shots", "gx"), None, None),
            P("shots"),
            P("shots"),
            P("shots"),
            P("shots", None),
            P(("shots", "gx")),
            P("gx", None),
            P(),
            P(),
            P(),
            P(),
            P(),
            P(),
        ),
        out_specs=(P("shots", None), P(("shots", "gx"), None, None, None)),
        check_vma=False,
    )
```

```python
import functools
import jax
import jax.numpy as jnp
import numpy as np
from jax import lax
from jax.experimental import pallas as pl
from jax.experimental.pallas import tpu as pltpu
from jax.sharding import PartitionSpec as P

MESH = pl.DeviceIdType.MESH
PAD = 8


def wave_kernel(
    n,
    c_ref,
    wave_prev,
    wave_now,
    adj_late,
    adj_last,
    wavelet,
    source,
    row_lane,
    z_lane,
    row_sub,
    z_sub,
    observed,
    grad_ref,
    wide_ref,
    resid_ref,
    fwd,
    adj,
    changes,
    c12,
    src,
    inj,
    hot,
    hot_t,
    zhot,
    zhot_t,
    parts,
    inj_parts,
    rec_send,
    rec_recv,
    resid8,
    f_send,
    f_recv,
    a_send,
    a_recv,
    r_send,
    r_recv,
    g_send,
    g_recv,
):
    cx, ny, nz = c_ref.shape
    steps = changes.shape[0]
    nrec = row_lane.shape[1]
    groups = nrec // 128
    rows = cx * ny
    me = lax.axis_index("gx")
    shot = lax.axis_index("shots")

    barrier = pltpu.get_barrier_semaphore()

    for buf in (fwd, adj):
        for k in range(3):
            buf[k] = jnp.zeros(buf.shape[1:], jnp.float32)
    wide_ref[0:2] = jnp.zeros((2, ny, nz), jnp.bfloat16)
    wide_ref[cx + 2 : cx + 4] = jnp.zeros((2, ny, nz), jnp.bfloat16)
    def greet(d, carry):
        pl.semaphore_signal(
            barrier, inc=1, device_id=(shot, lax.rem(me + d, n)), device_id_type=MESH
        )
        return carry

    lax.fori_loop(1, n, greet, 0)

    inner = pl.ds(PAD, ny)
    for i in range(cx):
        fwd[0, i + 2, inner] = wave_prev[i]
        fwd[1, i + 2, inner] = wave_now[i]
        adj[0, i + 2, inner] = adj_late[i]
        adj[1, i + 2, inner] = adj_last[i]
    pl.semaphore_wait(barrier, n - 1)

    def halo(buf, k, send, recv, up):
        lo = cx if up else 2
        to = 0 if up else cx + 2
        side = 1 if up else 0
        return pltpu.make_async_remote_copy(
            src_ref=buf.at[k, pl.ds(lo, 2), inner],
            dst_ref=buf.at[k, pl.ds(to, 2), inner],
            send_sem=send.at[side],
            recv_sem=recv.at[k, side],
            device_id=(shot, me + 1 if up else me - 1),
            device_id_type=MESH,
        )

    def start_side(buf, k, send, recv, up):
        @pl.when((me < n - 1) if up else (me > 0))
        def _():
            halo(buf, k, send, recv, up).start()

    def wait_side(buf, k, send, recv):
        @pl.when(me < n - 1)
        def _():
            halo(buf, k, send, recv, True).wait_send()
            halo(buf, k, send, recv, False).wait_recv()

        @pl.when(me > 0)
        def _():
            halo(buf, k, send, recv, False).wait_send()
            halo(buf, k, send, recv, True).wait_recv()

    for up in (False, True):
        start_side(fwd, 1, f_send, f_recv, up)
    for up in (False, True):
        start_side(adj, 1, a_send, a_recv, up)

    for i in range(cx):
        c12[i] = c_ref[i] * (1.0 / 12.0)
    y_at = lax.broadcasted_iota(jnp.int32, (ny, nz), 0)
    z_at = lax.broadcasted_iota(jnp.int32, (ny, nz), 1)
    for i in range(cx):
        flat = ((me * cx + i) * ny + y_at) * nz + z_at
        src[i] = jnp.where(flat == source[0], 1.0, 0.0)

    def build(j, carry):
        at = pl.ds(pl.multiple_of(j * 128, 128), 128)
        r_iota = lax.broadcasted_iota(jnp.int32, (128, nrec), 0) + j * 128
        hot[at, :] = jnp.where(r_iota == row_lane[...], 1.0, 0.0).astype(jnp.bfloat16)
        return carry

    lax.fori_loop(0, rows // 128, build, 0)

    def build_t(j, carry):
        at = pl.ds(pl.multiple_of(j * 128, 128), 128)
        r_iota = lax.broadcasted_iota(jnp.int32, (128, rows), 1)
        hot_t[at, :] = jnp.where(r_iota == row_sub[at, :], 1.0, 0.0).astype(jnp.bfloat16)
        lane = lax.broadcasted_iota(jnp.int32, (128, nz), 1)
        zhot[at, :] = jnp.where(lane == z_sub[at, :], 1.0, 0.0)
        return carry

    lax.fori_loop(0, groups, build_t, 0)
    zhot_t[...] = jnp.where(
        lax.broadcasted_iota(jnp.int32, (nz, nrec), 0) == z_lane[...], 1.0, 0.0
    )

    chunk = 32
    lane = lax.broadcasted_iota(jnp.int32, (chunk, nz), 1)

    def laplace12(buf, k, i, y):
        def at(plane, dy):
            return buf[k, plane, pl.ds(PAD + y + dy, chunk), :]

        mid = at(i + 2, 0)
        near = (at(i + 3, 0) + at(i + 1, 0)) + (at(i + 2, 1) + at(i + 2, -1))
        far = (at(i + 4, 0) + at(i, 0)) + (at(i + 2, 2) + at(i + 2, -2))
        near += jnp.where(lane >= 1, pltpu.roll(mid, 1, 1), 0.0)
        near += jnp.where(lane < nz - 1, pltpu.roll(mid, nz - 1, 1), 0.0)
        far += jnp.where(lane >= 2, pltpu.roll(mid, 2, 1), 0.0)
        far += jnp.where(lane < nz - 2, pltpu.roll(mid, nz - 2, 1), 0.0)
        return mid, 16.0 * near - far - 90.0 * mid

    order = [0, 1, cx - 2, cx - 1] + list(range(2, cx - 2))

    def send_records(t):
        def one(d, carry):
            pltpu.make_async_remote_copy(
                src_ref=rec_send.at[t],
                dst_ref=rec_recv.at[t, d - 1],
                send_sem=r_send.at[t],
                recv_sem=r_recv.at[t],
                device_id=(shot, lax.rem(me + d, n)),
                device_id_type=MESH,
            ).start()
            return carry

        lax.fori_loop(1, n, one, 0)

    def forward(t, carry):
        prev, cur, nxt = lax.rem(t, 3), lax.rem(t + 1, 3), lax.rem(t + 2, 3)
        impulse = wavelet[t]
        wait_side(fwd, cur, f_send, f_recv)
        for done, i in enumerate(order):
            for y in range(0, ny, chunk):
                mid, lap = laplace12(fwd, cur, i, y)
                at = pl.ds(y, chunk)
                change = c12[i, at] * lap + impulse * src[i, at]
                changes[t, i, at] = change
                newest = 2.0 * mid - fwd[prev, i + 2, pl.ds(PAD + y, chunk)] + change
                fwd[nxt, i + 2, pl.ds(PAD + y, chunk)] = newest
                high = newest.astype(jnp.bfloat16)
                parts[pl.ds(i * ny + y, chunk), 0:nz] = high
                parts[pl.ds(i * ny + y, chunk), nz : 2 * nz] = (
                    newest - high.astype(jnp.float32)
                ).astype(jnp.bfloat16)
            if done == 1:

                @pl.when(t < steps - 1)
                def _():
                    start_side(fwd, nxt, f_send, f_recv, False)

            if done == 3:

                @pl.when(t < steps - 1)
                def _():
                    start_side(fwd, nxt, f_send, f_recv, True)

        picked = jnp.dot(hot_t[...], parts[...], preferred_element_type=jnp.float32)
        zsel = zhot[...]
        ones = jnp.ones((8, nz), jnp.bfloat16)
        total = jnp.zeros((8, nrec), jnp.float32)
        for h in range(2):
            kept = (picked[:, h * nz : (h + 1) * nz] * zsel).astype(jnp.bfloat16)
            total += lax.dot_general(
                ones, kept, (((1,), (1,)), ((), ())), preferred_element_type=jnp.float32
            )
        for g in range(groups):
            rec_send[t, g : g + 1, :] = total[0:1, g * 128 : (g + 1) * 128]
        send_records(t)
        return carry

    lax.fori_loop(0, steps, forward, 0)

    for i in range(cx):
        grad_ref[i] = jnp.zeros((ny, nz), jnp.float32)

    def backward(s, carry):
        t = steps - 1 - s
        prev, cur, nxt = lax.rem(s, 3), lax.rem(s + 1, 3), lax.rem(s + 2, 3)
        arrived = rec_recv.at[t]
        pltpu.make_async_copy(arrived, arrived, r_recv.at[t]).wait()
        pltpu.make_async_copy(arrived, arrived, r_send.at[t]).wait()
        total = rec_send[t] + jnp.sum(rec_recv[t], axis=0)
        misfit = total - observed[t]
        resid_ref[t] = misfit
        resid8[...] = misfit
        for g in range(groups):
            at = pl.ds(g * 128, 128)
            value = zhot_t[:, at] * resid8[g : g + 1, :]
            high = value.astype(jnp.bfloat16)
            inj_parts[pl.ds(0, nz), at] = high
            inj_parts[pl.ds(nz, nz), at] = (value - high.astype(jnp.float32)).astype(jnp.bfloat16)
        spread = lax.dot_general(
            hot[...], inj_parts[...], (((1,), (1,)), ((), ())), preferred_element_type=jnp.float32
        )
        inj[...] = spread[:, 0:nz] + spread[:, nz : 2 * nz]
        wait_side(adj, cur, a_send, a_recv)
        for done, i in enumerate(order):
            for y in range(0, ny, chunk):
                mid, lap = laplace12(adj, cur, i, y)
                at = pl.ds(y, chunk)
                newest = (
                    2.0 * mid
                    - adj[prev, i + 2, pl.ds(PAD + y, chunk)]
                    + (c12[i, at] * lap + inj[pl.ds(i * ny + y, chunk), :])
                )
                adj[nxt, i + 2, pl.ds(PAD + y, chunk)] = newest
                grad_ref[i, at] = grad_ref[i, at] + newest * changes[t, i, at]
            if done == 1:

                @pl.when(s < steps - 1)
                def _():
                    start_side(adj, nxt, a_send, a_recv, False)

            if done == 3:

                @pl.when(s < steps - 1)
                def _():
                    start_side(adj, nxt, a_send, a_recv, True)

        return carry

    lax.fori_loop(0, steps, backward, 0)

    for i in range(cx):
        wide_ref[i + 2] = grad_ref[i].astype(jnp.bfloat16)

    def edge(up):
        side = 1 if up else 0
        return pltpu.make_async_remote_copy(
            src_ref=wide_ref.at[pl.ds(cx if up else 2, 2)],
            dst_ref=wide_ref.at[pl.ds(0 if up else cx + 2, 2)],
            send_sem=g_send.at[side],
            recv_sem=g_recv.at[side],
            device_id=(shot, me + 1 if up else me - 1),
            device_id_type=MESH,
        )

    @pl.when(me < n - 1)
    def _():
        edge(True).start()

    @pl.when(me > 0)
    def _():
        edge(False).start()

    @pl.when(me < n - 1)
    def _():
        edge(True).wait_send()
        edge(False).wait_recv()

    @pl.when(me > 0)
    def _():
        edge(False).wait_send()
        edge(True).wait_recv()


def wave(n, c, wave_prev, wave_now, adj_late, adj_last, wavelet, source, receivers, observed):
    cx, ny, nz = c.shape
    steps, nrec = observed.shape
    rows = cx * ny
    relative = receivers - lax.axis_index("gx") * (rows * nz)
    inside = (relative >= 0) & (relative < rows * nz)
    row = jnp.where(inside, relative // nz, -1)
    z = jnp.where(inside, relative % nz, -1)
    vmem = pl.BlockSpec(memory_space=pltpu.VMEM)
    smem = pl.BlockSpec(memory_space=pltpu.SMEM)
    groups = nrec // 128
    f32, bf16 = jnp.float32, jnp.bfloat16
    grad, wide, resid = pl.pallas_call(
        functools.partial(wave_kernel, n),
        out_shape=(
            jax.ShapeDtypeStruct((cx, ny, nz), f32),
            jax.ShapeDtypeStruct((cx + 4, ny, nz), bf16),
            jax.ShapeDtypeStruct((steps, groups, 128), f32),
        ),
        in_specs=[vmem] * 5 + [smem] * 2 + [vmem] * 5,
        out_specs=(vmem, vmem, vmem),
        scratch_shapes=[
            pltpu.VMEM((3, cx + 4, ny + 2 * PAD, nz), f32),
            pltpu.VMEM((3, cx + 4, ny + 2 * PAD, nz), f32),
            pltpu.VMEM((steps, cx, ny, nz), f32),
            pltpu.VMEM((cx, ny, nz), f32),
            pltpu.VMEM((cx, ny, nz), f32),
            pltpu.VMEM((rows, nz), f32),
            pltpu.VMEM((rows, nrec), bf16),
            pltpu.VMEM((nrec, rows), bf16),
            pltpu.VMEM((nrec, nz), f32),
            pltpu.VMEM((nz, nrec), f32),
            pltpu.VMEM((rows, 2 * nz), bf16),
            pltpu.VMEM((2 * nz, nrec), bf16),
            pltpu.VMEM((steps, groups, 128), f32),
            pltpu.VMEM((steps, n - 1, groups, 128), f32),
            pltpu.VMEM((groups, 128), f32),
            pltpu.SemaphoreType.DMA((2,)),
            pltpu.SemaphoreType.DMA((3, 2)),
            pltpu.SemaphoreType.DMA((2,)),
            pltpu.SemaphoreType.DMA((3, 2)),
            pltpu.SemaphoreType.DMA((steps,)),
            pltpu.SemaphoreType.DMA((steps,)),
            pltpu.SemaphoreType.DMA((2,)),
            pltpu.SemaphoreType.DMA((2,)),
        ],
        compiler_params=pltpu.CompilerParams(
            collective_id=0, has_side_effects=True, vmem_limit_bytes=56 * 2**20
        ),
        name="wave",
    )(
        c,
        wave_prev,
        wave_now,
        adj_late,
        adj_last,
        wavelet,
        source,
        row[None, :],
        z[None, :],
        row[:, None],
        z[:, None],
        observed.reshape(steps, groups, 128),
    )
    return grad, wide, resid.reshape(steps, nrec)


def prior_kernel(wide, grad, w1, w2, w3, b1, b2, b3, model_ref, planes, shifted, acc, bias1, bias2):
    cx, ny, nz = grad.shape
    deep = planes.shape[0] // ny
    span = 4
    planes[...] = jnp.zeros(planes.shape, jnp.float32)
    for x in range(cx + 4):
        planes[pl.ds(x, ny, stride=deep), :] = wide[x].astype(jnp.float32)
    shifted[0] = jnp.zeros(shifted.shape[1:], jnp.bfloat16)
    shifted[ny + 1] = jnp.zeros(shifted.shape[1:], jnp.bfloat16)
    acc[...] = jnp.zeros(acc.shape, jnp.float32)
    bias1[...] = jnp.broadcast_to(b1[...], bias1.shape)
    bias2[...] = jnp.broadcast_to(b2[...], bias2.shape)
    block = 8
    lane = lax.broadcasted_iota(jnp.int32, (block * deep, nz), 1)

    def shift(j, carry):
        v = planes[pl.ds(pl.multiple_of(j * block * deep, block * deep), block * deep), :]
        ahead = jnp.where(lane >= 1, pltpu.roll(v, 1, 1), 0.0)
        behind = jnp.where(lane < nz - 1, pltpu.roll(v, nz - 1, 1), 0.0)
        for c, part in enumerate((ahead, v, behind)):
            shifted[pl.ds(1 + j * block, block), c] = part.astype(jnp.bfloat16).reshape(
                block, deep, nz
            )
        return carry

    lax.fori_loop(0, ny // block, shift, 0)
    half = w2.shape[0]
    rest = w1.shape[0] - half
    small = lax.broadcasted_iota(jnp.int32, (cx, nz), 1)

    def rows(j, carry):
        y0 = j * span
        cells = jnp.concatenate(
            [shifted[pl.ds(y0 + k, 3)].reshape(9 * deep, nz) for k in range(span)], axis=1
        )
        lifted = jnp.dot(w1[...], cells, preferred_element_type=jnp.float32) + bias1[...]
        lifted = jnp.maximum(lifted, 0.0).astype(jnp.bfloat16)
        hidden = jnp.concatenate(
            [
                jnp.dot(w2[...], lifted[:half], preferred_element_type=jnp.float32),
                jnp.dot(w2[:rest, :rest], lifted[half:], preferred_element_type=jnp.float32),
            ],
            axis=0,
        )
        hidden = jnp.maximum(hidden + bias2[...], 0.0).astype(jnp.bfloat16)
        out = jnp.dot(w3[...], hidden, preferred_element_type=jnp.float32)
        for k in range(span):
            for b in range(3):
                c0, c1, c2 = [
                    out[(3 * b + c) * cx : (3 * b + c + 1) * cx, k * nz : (k + 1) * nz]
                    for c in range(3)
                ]
                total = c1 + jnp.where(small >= 1, pltpu.roll(c0, 1, 1), 0.0)
                total += jnp.where(small < nz - 1, pltpu.roll(c2, nz - 1, 1), 0.0)
                at = pl.ds(pl.multiple_of((y0 + k + 2 - b) * cx, cx), cx)
                acc[at, :] = acc[at, :] + total
        return carry

    lax.fori_loop(0, ny // span, rows, 0)
    for x in range(cx):
        conv = acc[pl.ds(cx + x, ny, stride=cx), :] + b3[0]
        model_ref[x] = (grad[x] + conv).astype(jnp.bfloat16)


def prior(wide, grad, weight_in, bias_in, weight_mix, bias_mix, weight_out, bias_out):
    cx, ny, nz = grad.shape
    ch = weight_in.shape[0]
    bf16, f32 = jnp.bfloat16, jnp.float32
    deep = 16
    held = cx + 2
    near = np.zeros((held, 3, deep), np.float32)
    far = np.zeros((cx, 3, held), np.float32)
    for a in range(3):
        for x in range(held):
            near[x, a, x + a] = 1.0
        for x in range(cx):
            far[x, a, x + a] = 1.0
    w1 = jnp.einsum("xai,hak->xhki", near.astype(bf16), weight_in.reshape(ch, 3, 9))
    w1 = w1.reshape(held * ch, 9 * deep)
    w2 = jnp.einsum("xi,hk->xhik", np.eye(cx, dtype=np.float32).astype(bf16), weight_mix)
    w2 = w2.reshape(cx * ch, cx * ch)
    margin = lax.axis_index("gx") * cx - 1 + jnp.arange(held, dtype=jnp.int32)
    keep = (margin >= 0) & (margin < cx * lax.axis_size("gx"))
    band = jnp.where(keep[None, None], far, 0.0).astype(bf16)
    w3 = jnp.einsum("xai,akh->kxih", band, weight_out.reshape(3, 9, ch))
    w3 = w3.reshape(9 * cx, held * ch)
    b1 = jnp.tile(bias_in, held)[:, None]
    b2 = jnp.tile(bias_mix, held)[:, None]
    vmem = pl.BlockSpec(memory_space=pltpu.VMEM)
    smem = pl.BlockSpec(memory_space=pltpu.SMEM)
    return pl.pallas_call(
        prior_kernel,
        out_shape=jax.ShapeDtypeStruct((cx, ny, nz), bf16),
        in_specs=[vmem] * 7 + [smem],
        out_specs=vmem,
        scratch_shapes=[
            pltpu.VMEM((ny * deep, nz), f32),
            pltpu.VMEM((ny + 2, 3, deep, nz), bf16),
            pltpu.VMEM(((ny + 2) * cx, nz), f32),
            pltpu.VMEM((held * ch, 4 * nz), f32),
            pltpu.VMEM((held * ch, 4 * nz), f32),
        ],
        compiler_params=pltpu.CompilerParams(vmem_limit_bytes=40 * 2**20),
        name="prior",
    )(wide, grad, w1.astype(bf16), w2.astype(bf16), w3.astype(bf16), b1, b2, bias_out)


def route_kernel(n, cap, model, owner_sub, owner_lane, print_lane, out, buckets, own, send, recv):
    cx, ny, nz = model.shape
    me = lax.axis_index("gx")
    shot = lax.axis_index("shots")
    barrier = pltpu.get_barrier_semaphore()

    def greet(d, carry):
        pl.semaphore_signal(
            barrier, inc=1, device_id=(shot, lax.rem(me + d, n)), device_id_type=MESH
        )
        return carry

    lax.fori_loop(1, n, greet, 0)
    before = lax.broadcasted_iota(jnp.int32, (ny, ny), 0)
    after = lax.broadcasted_iota(jnp.int32, (ny, ny), 1)
    same = jnp.where((owner_sub[...] == owner_lane[...]) & (before < after), 1.0, 0.0)
    slots = jnp.sum(same, axis=0, keepdims=True).astype(jnp.int32)
    place = owner_lane[...] * cap + slots
    place = jnp.where(print_lane[...] == 1, place, -1)
    at = lax.broadcasted_iota(jnp.int32, (n * cap, ny), 0)
    pick = jnp.where(at == place, 1.0, 0.0).astype(jnp.bfloat16)
    for x in range(cx):
        part = jnp.dot(pick, model[x], preferred_element_type=jnp.float32).astype(jnp.bfloat16)
        buckets[:, :, x * nz : (x + 1) * nz] = part.reshape(n, cap, nz)
    pl.semaphore_wait(barrier, n - 1)

    def copy(d):
        to = lax.rem(me + d, n)
        return pltpu.make_async_remote_copy(
            src_ref=buckets.at[to],
            dst_ref=out.at[me],
            send_sem=send.at[d],
            recv_sem=recv.at[d],
            device_id=(shot, to),
            device_id_type=MESH,
        )

    def landed(d):
        source = lax.rem(me - d + n, n)
        return pltpu.make_async_copy(out.at[source], out.at[source], recv.at[d])

    mine = pltpu.make_async_copy(buckets.at[me], out.at[me], own)

    def start(d, carry):
        copy(d).start()
        return carry

    def finish(d, carry):
        copy(d).wait_send()
        landed(d).wait()
        return carry

    lax.fori_loop(1, n, start, 0)
    mine.start()
    mine.wait()
    lax.fori_loop(1, n, finish, 0)


def route(n, cap, model, owner, footprint):
    cx, ny, nz = model.shape
    vmem = pl.BlockSpec(memory_space=pltpu.VMEM)
    return pl.pallas_call(
        functools.partial(route_kernel, n, cap),
        out_shape=jax.ShapeDtypeStruct((n, cap, cx * nz), jnp.bfloat16),
        in_specs=[vmem] * 4,
        out_specs=pl.BlockSpec(memory_space=pl.ANY),
        scratch_shapes=[
            pltpu.VMEM((n, cap, cx * nz), jnp.bfloat16),
            pltpu.SemaphoreType.DMA,
            pltpu.SemaphoreType.DMA((n,)),
            pltpu.SemaphoreType.DMA((n,)),
        ],
        compiler_params=pltpu.CompilerParams(
            collective_id=1, has_side_effects=True, vmem_limit_bytes=24 * 2**20
        ),
        name="route",
    )(model, owner, owner.reshape(1, ny), footprint.reshape(1, ny))


def per_device(
    courant_sq,
    wave_prev,
    wave_now,
    adj_late,
    adj_last,
    wavelet,
    source_cell,
    receivers,
    observed,
    footprint,
    brick_owner,
    prior_in,
    prior_in_bias,
    prior_mix,
    prior_mix_bias,
    prior_out,
    prior_out_bias,
):
    cells_x, cells_y, cells_z = wave_now.shape
    devices = lax.axis_size("gx")
    grad, grad_wide, residual_traces = wave(
        devices,
        courant_sq,
        wave_prev,
        wave_now,
        adj_late,
        adj_last,
        wavelet,
        source_cell,
        receivers,
        observed,
    )
    model_grad = prior(
        grad_wide,
        grad,
        prior_in,
        prior_in_bias,
        prior_mix,
        prior_mix_bias,
        prior_out,
        prior_out_bias,
    )
    capacity = max(2, 2 * cells_y // devices)
    if capacity % 16 == 0:
        arrived = route(devices, capacity, model_grad, brick_owner, footprint)
        return (residual_traces, arrived[None])
    bricks = model_grad.transpose(1, 0, 2).reshape(cells_y, cells_x * cells_z)
    bricks = jnp.where((footprint == 1)[:, None], bricks, jnp.zeros_like(bricks))
    owners = brick_owner[:, 0]
    same = owners[:, None] == owners[None, :]
    lower = (
        jnp.arange(cells_y, dtype=jnp.int32)[:, None]
        > jnp.arange(cells_y, dtype=jnp.int32)[None, :]
    )
    slots = jnp.sum((same & lower).astype(jnp.int32), axis=1)
    buckets = (
        jnp.zeros((devices, capacity, cells_x * cells_z), jnp.bfloat16)
        .at[owners, slots]
        .set(bricks)
    )
    arrived = lax.all_to_all(buckets, "gx", split_axis=0, concat_axis=0, tiled=True)
    return (residual_traces, arrived[None])


def solution(mesh):
    return jax.shard_map(
        per_device,
        mesh=mesh,
        in_specs=(
            P("gx", None, None),
            P(("shots", "gx"), None, None),
            P(("shots", "gx"), None, None),
            P(("shots", "gx"), None, None),
            P(("shots", "gx"), None, None),
            P("shots"),
            P("shots"),
            P("shots"),
            P("shots", None),
            P(("shots", "gx")),
            P("gx", None),
            P(),
            P(),
            P(),
            P(),
            P(),
            P(),
        ),
        out_specs=(P("shots", None), P(("shots", "gx"), None, None, None)),
        check_vma=False,
    )
```

```python
import functools
import jax
import jax.numpy as jnp
import numpy as np
from jax import lax
from jax.experimental import pallas as pl
from jax.experimental.pallas import tpu as pltpu
from jax.sharding import PartitionSpec as P

MESH = pl.DeviceIdType.MESH


def wave_kernel(
    n,
    c_ref,
    wave_prev,
    wave_now,
    adj_late,
    adj_last,
    wavelet,
    source,
    row_lane,
    z_lane,
    row_sub,
    z_sub,
    observed,
    grad_ref,
    wide_ref,
    resid_ref,
    fwd,
    adj,
    changes,
    c12,
    src,
    inj,
    hot,
    hot_t,
    zhot,
    zhot_t,
    parts,
    inj_parts,
    band_z,
    band_y,
    lap_yz,
    rec_send,
    rec_recv,
    resid8,
    f_send,
    f_recv,
    a_send,
    a_recv,
    r_send,
    r_recv,
    g_send,
    g_recv,
):
    cx, ny, nz = c_ref.shape
    steps = changes.shape[0]
    nrec = row_lane.shape[1]
    groups = nrec // 128
    rows = cx * ny
    me = lax.axis_index("gx")
    shot = lax.axis_index("shots")

    barrier = pltpu.get_barrier_semaphore()

    for buf in (fwd, adj):
        for k in range(1, 4):
            buf[k % 3, 0:2] = jnp.zeros((2, ny, nz), jnp.float32)
            buf[k % 3, cx + 2 : cx + 4] = jnp.zeros((2, ny, nz), jnp.float32)
    wide_ref[0:2] = jnp.zeros((2, ny, nz), jnp.bfloat16)
    wide_ref[cx + 2 : cx + 4] = jnp.zeros((2, ny, nz), jnp.bfloat16)
    def greet(d, carry):
        pl.semaphore_signal(
            barrier, inc=1, device_id=(shot, lax.rem(me + d, n)), device_id_type=MESH
        )
        return carry

    lax.fori_loop(1, n, greet, 0)

    for i in range(cx):
        fwd[0, i + 2] = wave_prev[i]
        fwd[1, i + 2] = wave_now[i]
        adj[0, i + 2] = adj_late[i]
        adj[1, i + 2] = adj_last[i]
    pl.semaphore_wait(barrier, n - 1)

    def halo(buf, k, send, recv, up):
        lo = cx if up else 2
        to = 0 if up else cx + 2
        side = 1 if up else 0
        return pltpu.make_async_remote_copy(
            src_ref=buf.at[k, pl.ds(lo, 2)],
            dst_ref=buf.at[k, pl.ds(to, 2)],
            send_sem=send.at[side],
            recv_sem=recv.at[k, side],
            device_id=(shot, me + 1 if up else me - 1),
            device_id_type=MESH,
        )

    def start_side(buf, k, send, recv, up):
        @pl.when((me < n - 1) if up else (me > 0))
        def _():
            halo(buf, k, send, recv, up).start()

    def wait_side(buf, k, send, recv):
        @pl.when(me < n - 1)
        def _():
            halo(buf, k, send, recv, True).wait_send()
            halo(buf, k, send, recv, False).wait_recv()

        @pl.when(me > 0)
        def _():
            halo(buf, k, send, recv, False).wait_send()
            halo(buf, k, send, recv, True).wait_recv()

    for up in (False, True):
        start_side(fwd, 1, f_send, f_recv, up)
    for up in (False, True):
        start_side(adj, 1, a_send, a_recv, up)

    for i in range(cx):
        c12[i] = c_ref[i] * (1.0 / 12.0)
    y_at = lax.broadcasted_iota(jnp.int32, (ny, nz), 0)
    z_at = lax.broadcasted_iota(jnp.int32, (ny, nz), 1)
    for i in range(cx):
        flat = ((me * cx + i) * ny + y_at) * nz + z_at
        src[i] = jnp.where(flat == source[0], 1.0, 0.0)

    def build(j, carry):
        at = pl.ds(pl.multiple_of(j * 128, 128), 128)
        r_iota = lax.broadcasted_iota(jnp.int32, (128, nrec), 0) + j * 128
        hot[at, :] = jnp.where(r_iota == row_lane[...], 1.0, 0.0).astype(jnp.bfloat16)
        return carry

    lax.fori_loop(0, rows // 128, build, 0)

    def build_t(j, carry):
        at = pl.ds(pl.multiple_of(j * 128, 128), 128)
        r_iota = lax.broadcasted_iota(jnp.int32, (128, rows), 1)
        hot_t[at, :] = jnp.where(r_iota == row_sub[at, :], 1.0, 0.0).astype(jnp.bfloat16)
        lane = lax.broadcasted_iota(jnp.int32, (128, nz), 1)
        zhot[at, :] = jnp.where(lane == z_sub[at, :], 1.0, 0.0)
        return carry

    lax.fori_loop(0, groups, build_t, 0)
    zhot_t[...] = jnp.where(
        lax.broadcasted_iota(jnp.int32, (nz, nrec), 0) == z_lane[...], 1.0, 0.0
    )

    across = lax.broadcasted_iota(jnp.int32, (2 * nz, nz), 0) % nz
    gap = jnp.abs(across - lax.broadcasted_iota(jnp.int32, (2 * nz, nz), 1))
    band_z[...] = (
        jnp.where(gap == 1, 16.0, 0.0) - jnp.where(gap == 2, 1.0, 0.0)
    ).astype(jnp.bfloat16)
    across = lax.broadcasted_iota(jnp.int32, (ny, 2 * ny), 1) % ny
    gap = jnp.abs(across - lax.broadcasted_iota(jnp.int32, (ny, 2 * ny), 0))
    band_y[...] = (
        jnp.where(gap == 1, 16.0, 0.0) - jnp.where(gap == 2, 1.0, 0.0)
    ).astype(jnp.bfloat16)

    chunk = 32

    def split(i, y, value):
        high = value.astype(jnp.bfloat16)
        at = pl.ds(i * ny + y, chunk)
        parts[at, 0:nz] = high
        parts[at, nz : 2 * nz] = (value - high.astype(jnp.float32)).astype(jnp.bfloat16)

    def along_yz(buf, k):
        for i in range(cx):
            at = pl.ds(i * ny, ny)
            z_part = jnp.dot(parts[at, :], band_z[...], preferred_element_type=jnp.float32)
            both = jnp.concatenate([parts[at, 0:nz], parts[at, nz : 2 * nz]], axis=0)
            y_part = jnp.dot(band_y[...], both, preferred_element_type=jnp.float32)
            lap_yz[i] = z_part + y_part - 90.0 * buf[k, i + 2]

    def lap_at(buf, k, i, y):
        at = pl.ds(y, chunk)
        near = buf[k, i + 3, at] + buf[k, i + 1, at]
        far = buf[k, i + 4, at] + buf[k, i, at]
        return buf[k, i + 2, at], lap_yz[i, at] + (16.0 * near - far)

    for i in range(cx):
        for y in range(0, ny, chunk):
            split(i, y, wave_now[i, pl.ds(y, chunk)])

    order = [0, 1, cx - 2, cx - 1] + list(range(2, cx - 2))

    def send_records(t):
        def one(d, carry):
            pltpu.make_async_remote_copy(
                src_ref=rec_send.at[t],
                dst_ref=rec_recv.at[t, d - 1],
                send_sem=r_send.at[t],
                recv_sem=r_recv.at[t],
                device_id=(shot, lax.rem(me + d, n)),
                device_id_type=MESH,
            ).start()
            return carry

        lax.fori_loop(1, n, one, 0)

    def forward(t, carry):
        prev, cur, nxt = lax.rem(t, 3), lax.rem(t + 1, 3), lax.rem(t + 2, 3)
        impulse = wavelet[t]
        along_yz(fwd, cur)
        wait_side(fwd, cur, f_send, f_recv)
        for done, i in enumerate(order):
            for y in range(0, ny, chunk):
                mid, lap = lap_at(fwd, cur, i, y)
                at = pl.ds(y, chunk)
                change = c12[i, at] * lap + impulse * src[i, at]
                changes[t, i, at] = change
                newest = 2.0 * mid - fwd[prev, i + 2, at] + change
                fwd[nxt, i + 2, at] = newest
                split(i, y, newest)
            if done == 1:

                @pl.when(t < steps - 1)
                def _():
                    start_side(fwd, nxt, f_send, f_recv, False)

            if done == 3:

                @pl.when(t < steps - 1)
                def _():
                    start_side(fwd, nxt, f_send, f_recv, True)

        picked = jnp.dot(hot_t[...], parts[...], preferred_element_type=jnp.float32)
        zsel = zhot[...]
        ones = jnp.ones((8, nz), jnp.bfloat16)
        total = jnp.zeros((8, nrec), jnp.float32)
        for h in range(2):
            kept = (picked[:, h * nz : (h + 1) * nz] * zsel).astype(jnp.bfloat16)
            total += lax.dot_general(
                ones, kept, (((1,), (1,)), ((), ())), preferred_element_type=jnp.float32
            )
        for g in range(groups):
            rec_send[t, g : g + 1, :] = total[0:1, g * 128 : (g + 1) * 128]
        send_records(t)
        return carry

    lax.fori_loop(0, steps, forward, 0)

    for i in range(cx):
        grad_ref[i] = jnp.zeros((ny, nz), jnp.float32)
        for y in range(0, ny, chunk):
            split(i, y, adj_last[i, pl.ds(y, chunk)])

    def backward(s, carry):
        t = steps - 1 - s
        prev, cur, nxt = lax.rem(s, 3), lax.rem(s + 1, 3), lax.rem(s + 2, 3)
        along_yz(adj, cur)
        arrived = rec_recv.at[t]
        pltpu.make_async_copy(arrived, arrived, r_recv.at[t]).wait()
        pltpu.make_async_copy(arrived, arrived, r_send.at[t]).wait()
        total = rec_send[t] + jnp.sum(rec_recv[t], axis=0)
        misfit = total - observed[t]
        resid_ref[t] = misfit
        resid8[...] = misfit
        for g in range(groups):
            at = pl.ds(g * 128, 128)
            value = zhot_t[:, at] * resid8[g : g + 1, :]
            high = value.astype(jnp.bfloat16)
            inj_parts[pl.ds(0, nz), at] = high
            inj_parts[pl.ds(nz, nz), at] = (value - high.astype(jnp.float32)).astype(jnp.bfloat16)
        spread = lax.dot_general(
            hot[...], inj_parts[...], (((1,), (1,)), ((), ())), preferred_element_type=jnp.float32
        )
        inj[...] = spread[:, 0:nz] + spread[:, nz : 2 * nz]
        wait_side(adj, cur, a_send, a_recv)
        for done, i in enumerate(order):
            for y in range(0, ny, chunk):
                mid, lap = lap_at(adj, cur, i, y)
                at = pl.ds(y, chunk)
                newest = (
                    2.0 * mid
                    - adj[prev, i + 2, at]
                    + (c12[i, at] * lap + inj[pl.ds(i * ny + y, chunk), :])
                )
                adj[nxt, i + 2, at] = newest
                split(i, y, newest)
                grad_ref[i, at] = grad_ref[i, at] + newest * changes[t, i, at]
            if done == 1:

                @pl.when(s < steps - 1)
                def _():
                    start_side(adj, nxt, a_send, a_recv, False)

            if done == 3:

                @pl.when(s < steps - 1)
                def _():
                    start_side(adj, nxt, a_send, a_recv, True)

        return carry

    lax.fori_loop(0, steps, backward, 0)

    for i in range(cx):
        wide_ref[i + 2] = grad_ref[i].astype(jnp.bfloat16)

    def edge(up):
        side = 1 if up else 0
        return pltpu.make_async_remote_copy(
            src_ref=wide_ref.at[pl.ds(cx if up else 2, 2)],
            dst_ref=wide_ref.at[pl.ds(0 if up else cx + 2, 2)],
            send_sem=g_send.at[side],
            recv_sem=g_recv.at[side],
            device_id=(shot, me + 1 if up else me - 1),
            device_id_type=MESH,
        )

    @pl.when(me < n - 1)
    def _():
        edge(True).start()

    @pl.when(me > 0)
    def _():
        edge(False).start()

    @pl.when(me < n - 1)
    def _():
        edge(True).wait_send()
        edge(False).wait_recv()

    @pl.when(me > 0)
    def _():
        edge(False).wait_send()
        edge(True).wait_recv()


def wave(n, c, wave_prev, wave_now, adj_late, adj_last, wavelet, source, receivers, observed):
    cx, ny, nz = c.shape
    steps, nrec = observed.shape
    rows = cx * ny
    relative = receivers - lax.axis_index("gx") * (rows * nz)
    inside = (relative >= 0) & (relative < rows * nz)
    row = jnp.where(inside, relative // nz, -1)
    z = jnp.where(inside, relative % nz, -1)
    vmem = pl.BlockSpec(memory_space=pltpu.VMEM)
    smem = pl.BlockSpec(memory_space=pltpu.SMEM)
    groups = nrec // 128
    f32, bf16 = jnp.float32, jnp.bfloat16
    grad, wide, resid = pl.pallas_call(
        functools.partial(wave_kernel, n),
        out_shape=(
            jax.ShapeDtypeStruct((cx, ny, nz), f32),
            jax.ShapeDtypeStruct((cx + 4, ny, nz), bf16),
            jax.ShapeDtypeStruct((steps, groups, 128), f32),
        ),
        in_specs=[vmem] * 5 + [smem] * 2 + [vmem] * 5,
        out_specs=(vmem, vmem, vmem),
        scratch_shapes=[
            pltpu.VMEM((3, cx + 4, ny, nz), f32),
            pltpu.VMEM((3, cx + 4, ny, nz), f32),
            pltpu.VMEM((steps, cx, ny, nz), f32),
            pltpu.VMEM((cx, ny, nz), f32),
            pltpu.VMEM((cx, ny, nz), f32),
            pltpu.VMEM((rows, nz), f32),
            pltpu.VMEM((rows, nrec), bf16),
            pltpu.VMEM((nrec, rows), bf16),
            pltpu.VMEM((nrec, nz), f32),
            pltpu.VMEM((nz, nrec), f32),
            pltpu.VMEM((rows, 2 * nz), bf16),
            pltpu.VMEM((2 * nz, nrec), bf16),
            pltpu.VMEM((2 * nz, nz), bf16),
            pltpu.VMEM((ny, 2 * ny), bf16),
            pltpu.VMEM((cx, ny, nz), f32),
            pltpu.VMEM((steps, groups, 128), f32),
            pltpu.VMEM((steps, n - 1, groups, 128), f32),
            pltpu.VMEM((groups, 128), f32),
            pltpu.SemaphoreType.DMA((2,)),
            pltpu.SemaphoreType.DMA((3, 2)),
            pltpu.SemaphoreType.DMA((2,)),
            pltpu.SemaphoreType.DMA((3, 2)),
            pltpu.SemaphoreType.DMA((steps,)),
            pltpu.SemaphoreType.DMA((steps,)),
            pltpu.SemaphoreType.DMA((2,)),
            pltpu.SemaphoreType.DMA((2,)),
        ],
        compiler_params=pltpu.CompilerParams(
            collective_id=0, has_side_effects=True, vmem_limit_bytes=56 * 2**20
        ),
        name="wave",
    )(
        c,
        wave_prev,
        wave_now,
        adj_late,
        adj_last,
        wavelet,
        source,
        row[None, :],
        z[None, :],
        row[:, None],
        z[:, None],
        observed.reshape(steps, groups, 128),
    )
    return grad, wide, resid.reshape(steps, nrec)


def prior_kernel(wide, grad, w1, w2, w3, b1, b2, b3, model_ref, planes, shifted, acc, bias1, bias2):
    cx, ny, nz = grad.shape
    deep = planes.shape[0] // ny
    span = 4
    planes[...] = jnp.zeros(planes.shape, jnp.float32)
    for x in range(cx + 4):
        planes[pl.ds(x, ny, stride=deep), :] = wide[x].astype(jnp.float32)
    shifted[0] = jnp.zeros(shifted.shape[1:], jnp.bfloat16)
    shifted[ny + 1] = jnp.zeros(shifted.shape[1:], jnp.bfloat16)
    acc[...] = jnp.zeros(acc.shape, jnp.float32)
    bias1[...] = jnp.broadcast_to(b1[...], bias1.shape)
    bias2[...] = jnp.broadcast_to(b2[...], bias2.shape)
    block = 8
    lane = lax.broadcasted_iota(jnp.int32, (block * deep, nz), 1)

    def shift(j, carry):
        v = planes[pl.ds(pl.multiple_of(j * block * deep, block * deep), block * deep), :]
        ahead = jnp.where(lane >= 1, pltpu.roll(v, 1, 1), 0.0)
        behind = jnp.where(lane < nz - 1, pltpu.roll(v, nz - 1, 1), 0.0)
        for c, part in enumerate((ahead, v, behind)):
            shifted[pl.ds(1 + j * block, block), c] = part.astype(jnp.bfloat16).reshape(
                block, deep, nz
            )
        return carry

    lax.fori_loop(0, ny // block, shift, 0)
    half = w2.shape[0]
    rest = w1.shape[0] - half
    small = lax.broadcasted_iota(jnp.int32, (cx, nz), 1)

    def rows(j, carry):
        y0 = j * span
        cells = jnp.concatenate(
            [shifted[pl.ds(y0 + k, 3)].reshape(9 * deep, nz) for k in range(span)], axis=1
        )
        lifted = jnp.dot(w1[...], cells, preferred_element_type=jnp.float32) + bias1[...]
        lifted = jnp.maximum(lifted, 0.0).astype(jnp.bfloat16)
        hidden = jnp.concatenate(
            [
                jnp.dot(w2[...], lifted[:half], preferred_element_type=jnp.float32),
                jnp.dot(w2[:rest, :rest], lifted[half:], preferred_element_type=jnp.float32),
            ],
            axis=0,
        )
        hidden = jnp.maximum(hidden + bias2[...], 0.0).astype(jnp.bfloat16)
        out = jnp.dot(w3[...], hidden, preferred_element_type=jnp.float32)
        for k in range(span):
            for b in range(3):
                c0, c1, c2 = [
                    out[(3 * b + c) * cx : (3 * b + c + 1) * cx, k * nz : (k + 1) * nz]
                    for c in range(3)
                ]
                total = c1 + jnp.where(small >= 1, pltpu.roll(c0, 1, 1), 0.0)
                total += jnp.where(small < nz - 1, pltpu.roll(c2, nz - 1, 1), 0.0)
                at = pl.ds(pl.multiple_of((y0 + k + 2 - b) * cx, cx), cx)
                acc[at, :] = acc[at, :] + total
        return carry

    lax.fori_loop(0, ny // span, rows, 0)
    for x in range(cx):
        conv = acc[pl.ds(cx + x, ny, stride=cx), :] + b3[0]
        model_ref[x] = (grad[x] + conv).astype(jnp.bfloat16)


def prior(wide, grad, weight_in, bias_in, weight_mix, bias_mix, weight_out, bias_out):
    cx, ny, nz = grad.shape
    ch = weight_in.shape[0]
    bf16, f32 = jnp.bfloat16, jnp.float32
    deep = 16
    held = cx + 2
    near = np.zeros((held, 3, deep), np.float32)
    far = np.zeros((cx, 3, held), np.float32)
    for a in range(3):
        for x in range(held):
            near[x, a, x + a] = 1.0
        for x in range(cx):
            far[x, a, x + a] = 1.0
    w1 = jnp.einsum("xai,hak->xhki", near.astype(bf16), weight_in.reshape(ch, 3, 9))
    w1 = w1.reshape(held * ch, 9 * deep)
    w2 = jnp.einsum("xi,hk->xhik", np.eye(cx, dtype=np.float32).astype(bf16), weight_mix)
    w2 = w2.reshape(cx * ch, cx * ch)
    margin = lax.axis_index("gx") * cx - 1 + jnp.arange(held, dtype=jnp.int32)
    keep = (margin >= 0) & (margin < cx * lax.axis_size("gx"))
    band = jnp.where(keep[None, None], far, 0.0).astype(bf16)
    w3 = jnp.einsum("xai,akh->kxih", band, weight_out.reshape(3, 9, ch))
    w3 = w3.reshape(9 * cx, held * ch)
    b1 = jnp.tile(bias_in, held)[:, None]
    b2 = jnp.tile(bias_mix, held)[:, None]
    vmem = pl.BlockSpec(memory_space=pltpu.VMEM)
    smem = pl.BlockSpec(memory_space=pltpu.SMEM)
    return pl.pallas_call(
        prior_kernel,
        out_shape=jax.ShapeDtypeStruct((cx, ny, nz), bf16),
        in_specs=[vmem] * 7 + [smem],
        out_specs=vmem,
        scratch_shapes=[
            pltpu.VMEM((ny * deep, nz), f32),
            pltpu.VMEM((ny + 2, 3, deep, nz), bf16),
            pltpu.VMEM(((ny + 2) * cx, nz), f32),
            pltpu.VMEM((held * ch, 4 * nz), f32),
            pltpu.VMEM((held * ch, 4 * nz), f32),
        ],
        compiler_params=pltpu.CompilerParams(vmem_limit_bytes=40 * 2**20),
        name="prior",
    )(wide, grad, w1.astype(bf16), w2.astype(bf16), w3.astype(bf16), b1, b2, bias_out)


def route_kernel(n, cap, model, owner_sub, owner_lane, print_lane, out, buckets, own, send, recv):
    cx, ny, nz = model.shape
    me = lax.axis_index("gx")
    shot = lax.axis_index("shots")
    barrier = pltpu.get_barrier_semaphore()

    def greet(d, carry):
        pl.semaphore_signal(
            barrier, inc=1, device_id=(shot, lax.rem(me + d, n)), device_id_type=MESH
        )
        return carry

    lax.fori_loop(1, n, greet, 0)
    before = lax.broadcasted_iota(jnp.int32, (ny, ny), 0)
    after = lax.broadcasted_iota(jnp.int32, (ny, ny), 1)
    same = jnp.where((owner_sub[...] == owner_lane[...]) & (before < after), 1.0, 0.0)
    slots = jnp.sum(same, axis=0, keepdims=True).astype(jnp.int32)
    place = owner_lane[...] * cap + slots
    place = jnp.where(print_lane[...] == 1, place, -1)
    at = lax.broadcasted_iota(jnp.int32, (n * cap, ny), 0)
    pick = jnp.where(at == place, 1.0, 0.0).astype(jnp.bfloat16)
    for x in range(cx):
        part = jnp.dot(pick, model[x], preferred_element_type=jnp.float32).astype(jnp.bfloat16)
        buckets[:, :, x * nz : (x + 1) * nz] = part.reshape(n, cap, nz)
    pl.semaphore_wait(barrier, n - 1)

    def copy(d):
        to = lax.rem(me + d, n)
        return pltpu.make_async_remote_copy(
            src_ref=buckets.at[to],
            dst_ref=out.at[me],
            send_sem=send.at[d],
            recv_sem=recv.at[d],
            device_id=(shot, to),
            device_id_type=MESH,
        )

    def landed(d):
        source = lax.rem(me - d + n, n)
        return pltpu.make_async_copy(out.at[source], out.at[source], recv.at[d])

    mine = pltpu.make_async_copy(buckets.at[me], out.at[me], own)

    def start(d, carry):
        copy(d).start()
        return carry

    def finish(d, carry):
        copy(d).wait_send()
        landed(d).wait()
        return carry

    lax.fori_loop(1, n, start, 0)
    mine.start()
    mine.wait()
    lax.fori_loop(1, n, finish, 0)


def route(n, cap, model, owner, footprint):
    cx, ny, nz = model.shape
    vmem = pl.BlockSpec(memory_space=pltpu.VMEM)
    return pl.pallas_call(
        functools.partial(route_kernel, n, cap),
        out_shape=jax.ShapeDtypeStruct((n, cap, cx * nz), jnp.bfloat16),
        in_specs=[vmem] * 4,
        out_specs=pl.BlockSpec(memory_space=pl.ANY),
        scratch_shapes=[
            pltpu.VMEM((n, cap, cx * nz), jnp.bfloat16),
            pltpu.SemaphoreType.DMA,
            pltpu.SemaphoreType.DMA((n,)),
            pltpu.SemaphoreType.DMA((n,)),
        ],
        compiler_params=pltpu.CompilerParams(
            collective_id=1, has_side_effects=True, vmem_limit_bytes=24 * 2**20
        ),
        name="route",
    )(model, owner, owner.reshape(1, ny), footprint.reshape(1, ny))


def per_device(
    courant_sq,
    wave_prev,
    wave_now,
    adj_late,
    adj_last,
    wavelet,
    source_cell,
    receivers,
    observed,
    footprint,
    brick_owner,
    prior_in,
    prior_in_bias,
    prior_mix,
    prior_mix_bias,
    prior_out,
    prior_out_bias,
):
    cells_x, cells_y, cells_z = wave_now.shape
    devices = lax.axis_size("gx")
    grad, grad_wide, residual_traces = wave(
        devices,
        courant_sq,
        wave_prev,
        wave_now,
        adj_late,
        adj_last,
        wavelet,
        source_cell,
        receivers,
        observed,
    )
    model_grad = prior(
        grad_wide,
        grad,
        prior_in,
        prior_in_bias,
        prior_mix,
        prior_mix_bias,
        prior_out,
        prior_out_bias,
    )
    capacity = max(2, 2 * cells_y // devices)
    if capacity % 16 == 0:
        arrived = route(devices, capacity, model_grad, brick_owner, footprint)
        return (residual_traces, arrived[None])
    bricks = model_grad.transpose(1, 0, 2).reshape(cells_y, cells_x * cells_z)
    bricks = jnp.where((footprint == 1)[:, None], bricks, jnp.zeros_like(bricks))
    owners = brick_owner[:, 0]
    same = owners[:, None] == owners[None, :]
    lower = (
        jnp.arange(cells_y, dtype=jnp.int32)[:, None]
        > jnp.arange(cells_y, dtype=jnp.int32)[None, :]
    )
    slots = jnp.sum((same & lower).astype(jnp.int32), axis=1)
    buckets = (
        jnp.zeros((devices, capacity, cells_x * cells_z), jnp.bfloat16)
        .at[owners, slots]
        .set(bricks)
    )
    arrived = lax.all_to_all(buckets, "gx", split_axis=0, concat_axis=0, tiled=True)
    return (residual_traces, arrived[None])


def solution(mesh):
    return jax.shard_map(
        per_device,
        mesh=mesh,
        in_specs=(
            P("gx", None, None),
            P(("shots", "gx"), None, None),
            P(("shots", "gx"), None, None),
            P(("shots", "gx"), None, None),
            P(("shots", "gx"), None, None),
            P("shots"),
            P("shots"),
            P("shots"),
            P("shots", None),
            P(("shots", "gx")),
            P("gx", None),
            P(),
            P(),
            P(),
            P(),
            P(),
            P(),
        ),
        out_specs=(P("shots", None), P(("shots", "gx"), None, None, None)),
        check_vma=False,
    )
```

```python
import functools
import jax
import jax.numpy as jnp
import numpy as np
from jax import lax
from jax.experimental import pallas as pl
from jax.experimental.pallas import tpu as pltpu
from jax.sharding import PartitionSpec as P

MESH = pl.DeviceIdType.MESH


def wave_kernel(
    n,
    c_ref,
    wave_prev,
    wave_now,
    adj_late,
    adj_last,
    wavelet,
    source,
    row_lane,
    z_lane,
    row_sub,
    z_sub,
    observed,
    grad_ref,
    wide_ref,
    resid_ref,
    fwd,
    adj,
    changes,
    c12,
    src,
    inj,
    hot,
    hot_t,
    zhot,
    zhot_t,
    parts,
    inj_parts,
    band_z,
    band_y,
    lap_yz,
    rec_send,
    rec_recv,
    resid8,
    f_send,
    f_recv,
    a_send,
    a_recv,
    r_send,
    r_recv,
    g_send,
    g_recv,
):
    cx, ny, nz = c_ref.shape
    steps = changes.shape[0]
    nrec = row_lane.shape[1]
    groups = nrec // 128
    rows = cx * ny
    me = lax.axis_index("gx")
    shot = lax.axis_index("shots")

    barrier = pltpu.get_barrier_semaphore()

    for buf in (fwd, adj):
        for k in range(1, 4):
            buf[k % 3, 0:2] = jnp.zeros((2, ny, nz), jnp.float32)
            buf[k % 3, cx + 2 : cx + 4] = jnp.zeros((2, ny, nz), jnp.float32)
    wide_ref[0:2] = jnp.zeros((2, ny, nz), jnp.bfloat16)
    wide_ref[cx + 2 : cx + 4] = jnp.zeros((2, ny, nz), jnp.bfloat16)
    def greet(d, carry):
        pl.semaphore_signal(
            barrier, inc=1, device_id=(shot, lax.rem(me + d, n)), device_id_type=MESH
        )
        return carry

    lax.fori_loop(1, n, greet, 0)

    for i in range(cx):
        fwd[0, i + 2] = wave_prev[i]
        fwd[1, i + 2] = wave_now[i]
        adj[0, i + 2] = adj_late[i]
        adj[1, i + 2] = adj_last[i]
    pl.semaphore_wait(barrier, n - 1)

    def halo(buf, k, send, recv, up, plane):
        lo = cx if up else 2
        to = 0 if up else cx + 2
        side = 1 if up else 0
        return pltpu.make_async_remote_copy(
            src_ref=buf.at[k, lo + plane],
            dst_ref=buf.at[k, to + plane],
            send_sem=send.at[side, plane],
            recv_sem=recv.at[k, side, plane],
            device_id=(shot, me + 1 if up else me - 1),
            device_id_type=MESH,
        )

    def start_side(buf, k, send, recv, up, plane):
        @pl.when((me < n - 1) if up else (me > 0))
        def _():
            halo(buf, k, send, recv, up, plane).start()

    def wait_side(buf, k, send, recv, low):
        @pl.when((me > 0) if low else (me < n - 1))
        def _():
            for plane in range(2):
                halo(buf, k, send, recv, not low, plane).wait_send()
                halo(buf, k, send, recv, low, plane).wait_recv()

    for buf, send, recv in ((fwd, f_send, f_recv), (adj, a_send, a_recv)):
        for up in (False, True):
            for plane in range(2):
                start_side(buf, 1, send, recv, up, plane)

    for i in range(cx):
        c12[i] = c_ref[i] * (1.0 / 12.0)
    y_at = lax.broadcasted_iota(jnp.int32, (ny, nz), 0)
    z_at = lax.broadcasted_iota(jnp.int32, (ny, nz), 1)
    for i in range(cx):
        flat = ((me * cx + i) * ny + y_at) * nz + z_at
        src[i] = jnp.where(flat == source[0], 1.0, 0.0)

    def build(j, carry):
        at = pl.ds(pl.multiple_of(j * 128, 128), 128)
        r_iota = lax.broadcasted_iota(jnp.int32, (128, nrec), 0) + j * 128
        hot[at, :] = jnp.where(r_iota == row_lane[...], 1.0, 0.0).astype(jnp.bfloat16)
        return carry

    lax.fori_loop(0, rows // 128, build, 0)

    def build_t(j, carry):
        at = pl.ds(pl.multiple_of(j * 128, 128), 128)
        r_iota = lax.broadcasted_iota(jnp.int32, (128, rows), 1)
        hot_t[at, :] = jnp.where(r_iota == row_sub[at, :], 1.0, 0.0).astype(jnp.bfloat16)
        lane = lax.broadcasted_iota(jnp.int32, (128, nz), 1)
        zhot[at, :] = jnp.where(lane == z_sub[at, :], 1.0, 0.0)
        return carry

    lax.fori_loop(0, groups, build_t, 0)
    zhot_t[...] = jnp.where(
        lax.broadcasted_iota(jnp.int32, (nz, nrec), 0) == z_lane[...], 1.0, 0.0
    )

    across = lax.broadcasted_iota(jnp.int32, (2 * nz, nz), 0) % nz
    gap = jnp.abs(across - lax.broadcasted_iota(jnp.int32, (2 * nz, nz), 1))
    band_z[...] = (
        jnp.where(gap == 1, 16.0, 0.0) - jnp.where(gap == 2, 1.0, 0.0)
    ).astype(jnp.bfloat16)
    across = lax.broadcasted_iota(jnp.int32, (ny, 2 * ny), 1) % ny
    gap = jnp.abs(across - lax.broadcasted_iota(jnp.int32, (ny, 2 * ny), 0))
    band_y[...] = (
        jnp.where(gap == 1, 16.0, 0.0) - jnp.where(gap == 2, 1.0, 0.0)
    ).astype(jnp.bfloat16)

    chunk = 32

    def split(i, y, value):
        high = value.astype(jnp.bfloat16)
        at = pl.ds(i * ny + y, chunk)
        parts[at, 0:nz] = high
        parts[at, nz : 2 * nz] = (value - high.astype(jnp.float32)).astype(jnp.bfloat16)

    def along_yz(buf, k):
        for i in range(cx):
            at = pl.ds(i * ny, ny)
            z_part = jnp.dot(parts[at, :], band_z[...], preferred_element_type=jnp.float32)
            both = jnp.concatenate([parts[at, 0:nz], parts[at, nz : 2 * nz]], axis=0)
            y_part = jnp.dot(band_y[...], both, preferred_element_type=jnp.float32)
            lap_yz[i] = z_part + y_part - 90.0 * buf[k, i + 2]

    def lap_at(buf, k, i, y):
        at = pl.ds(y, chunk)
        near = buf[k, i + 3, at] + buf[k, i + 1, at]
        far = buf[k, i + 4, at] + buf[k, i, at]
        return buf[k, i + 2, at], lap_yz[i, at] + (16.0 * near - far)

    for i in range(cx):
        for y in range(0, ny, chunk):
            split(i, y, wave_now[i, pl.ds(y, chunk)])

    order = [0, 1, cx - 2, cx - 1] + list(range(2, cx - 2))

    def send_records(t):
        def one(d, carry):
            pltpu.make_async_remote_copy(
                src_ref=rec_send.at[t],
                dst_ref=rec_recv.at[t, d - 1],
                send_sem=r_send.at[t],
                recv_sem=r_recv.at[t],
                device_id=(shot, lax.rem(me + d, n)),
                device_id_type=MESH,
            ).start()
            return carry

        lax.fori_loop(1, n, one, 0)

    def forward(t, carry):
        prev, cur, nxt = lax.rem(t, 3), lax.rem(t + 1, 3), lax.rem(t + 2, 3)
        impulse = wavelet[t]
        along_yz(fwd, cur)
        for done, i in enumerate(order):
            if done == 0 or done == 2:
                wait_side(fwd, cur, f_send, f_recv, done == 0)
            for y in range(0, ny, chunk):
                mid, lap = lap_at(fwd, cur, i, y)
                at = pl.ds(y, chunk)
                change = c12[i, at] * lap + impulse * src[i, at]
                changes[t, i, at] = change
                newest = 2.0 * mid - fwd[prev, i + 2, at] + change
                fwd[nxt, i + 2, at] = newest
                split(i, y, newest)
            if done < 4:

                @pl.when(t < steps - 1)
                def _():
                    start_side(fwd, nxt, f_send, f_recv, done >= 2, done % 2)

        picked = jnp.dot(hot_t[...], parts[...], preferred_element_type=jnp.float32)
        zsel = zhot[...]
        ones = jnp.ones((8, nz), jnp.bfloat16)
        total = jnp.zeros((8, nrec), jnp.float32)
        for h in range(2):
            kept = (picked[:, h * nz : (h + 1) * nz] * zsel).astype(jnp.bfloat16)
            total += lax.dot_general(
                ones, kept, (((1,), (1,)), ((), ())), preferred_element_type=jnp.float32
            )
        for g in range(groups):
            rec_send[t, g : g + 1, :] = total[0:1, g * 128 : (g + 1) * 128]
        send_records(t)
        return carry

    lax.fori_loop(0, steps, forward, 0)

    for i in range(cx):
        grad_ref[i] = jnp.zeros((ny, nz), jnp.float32)
        for y in range(0, ny, chunk):
            split(i, y, adj_last[i, pl.ds(y, chunk)])

    def backward(s, carry):
        t = steps - 1 - s
        prev, cur, nxt = lax.rem(s, 3), lax.rem(s + 1, 3), lax.rem(s + 2, 3)
        along_yz(adj, cur)
        arrived = rec_recv.at[t]
        pltpu.make_async_copy(arrived, arrived, r_recv.at[t]).wait()
        pltpu.make_async_copy(arrived, arrived, r_send.at[t]).wait()
        total = rec_send[t] + jnp.sum(rec_recv[t], axis=0)
        misfit = total - observed[t]
        resid_ref[t] = misfit
        resid8[...] = misfit
        for g in range(groups):
            at = pl.ds(g * 128, 128)
            value = zhot_t[:, at] * resid8[g : g + 1, :]
            high = value.astype(jnp.bfloat16)
            inj_parts[pl.ds(0, nz), at] = high
            inj_parts[pl.ds(nz, nz), at] = (value - high.astype(jnp.float32)).astype(jnp.bfloat16)
        spread = lax.dot_general(
            hot[...], inj_parts[...], (((1,), (1,)), ((), ())), preferred_element_type=jnp.float32
        )
        inj[...] = spread[:, 0:nz] + spread[:, nz : 2 * nz]
        for done, i in enumerate(order):
            if done == 0 or done == 2:
                wait_side(adj, cur, a_send, a_recv, done == 0)
            for y in range(0, ny, chunk):
                mid, lap = lap_at(adj, cur, i, y)
                at = pl.ds(y, chunk)
                newest = (
                    2.0 * mid
                    - adj[prev, i + 2, at]
                    + (c12[i, at] * lap + inj[pl.ds(i * ny + y, chunk), :])
                )
                adj[nxt, i + 2, at] = newest
                split(i, y, newest)
                grad_ref[i, at] = grad_ref[i, at] + newest * changes[t, i, at]
            if done < 4:

                @pl.when(s < steps - 1)
                def _():
                    start_side(adj, nxt, a_send, a_recv, done >= 2, done % 2)

        return carry

    lax.fori_loop(0, steps, backward, 0)

    for i in range(cx):
        wide_ref[i + 2] = grad_ref[i].astype(jnp.bfloat16)

    def edge(up):
        side = 1 if up else 0
        return pltpu.make_async_remote_copy(
            src_ref=wide_ref.at[pl.ds(cx if up else 2, 2)],
            dst_ref=wide_ref.at[pl.ds(0 if up else cx + 2, 2)],
            send_sem=g_send.at[side],
            recv_sem=g_recv.at[side],
            device_id=(shot, me + 1 if up else me - 1),
            device_id_type=MESH,
        )

    @pl.when(me < n - 1)
    def _():
        edge(True).start()

    @pl.when(me > 0)
    def _():
        edge(False).start()

    @pl.when(me < n - 1)
    def _():
        edge(True).wait_send()
        edge(False).wait_recv()

    @pl.when(me > 0)
    def _():
        edge(False).wait_send()
        edge(True).wait_recv()


def wave(n, c, wave_prev, wave_now, adj_late, adj_last, wavelet, source, receivers, observed):
    cx, ny, nz = c.shape
    steps, nrec = observed.shape
    rows = cx * ny
    relative = receivers - lax.axis_index("gx") * (rows * nz)
    inside = (relative >= 0) & (relative < rows * nz)
    row = jnp.where(inside, relative // nz, -1)
    z = jnp.where(inside, relative % nz, -1)
    vmem = pl.BlockSpec(memory_space=pltpu.VMEM)
    smem = pl.BlockSpec(memory_space=pltpu.SMEM)
    groups = nrec // 128
    f32, bf16 = jnp.float32, jnp.bfloat16
    grad, wide, resid = pl.pallas_call(
        functools.partial(wave_kernel, n),
        out_shape=(
            jax.ShapeDtypeStruct((cx, ny, nz), f32),
            jax.ShapeDtypeStruct((cx + 4, ny, nz), bf16),
            jax.ShapeDtypeStruct((steps, groups, 128), f32),
        ),
        in_specs=[vmem] * 5 + [smem] * 2 + [vmem] * 5,
        out_specs=(vmem, vmem, vmem),
        scratch_shapes=[
            pltpu.VMEM((3, cx + 4, ny, nz), f32),
            pltpu.VMEM((3, cx + 4, ny, nz), f32),
            pltpu.VMEM((steps, cx, ny, nz), f32),
            pltpu.VMEM((cx, ny, nz), f32),
            pltpu.VMEM((cx, ny, nz), f32),
            pltpu.VMEM((rows, nz), f32),
            pltpu.VMEM((rows, nrec), bf16),
            pltpu.VMEM((nrec, rows), bf16),
            pltpu.VMEM((nrec, nz), f32),
            pltpu.VMEM((nz, nrec), f32),
            pltpu.VMEM((rows, 2 * nz), bf16),
            pltpu.VMEM((2 * nz, nrec), bf16),
            pltpu.VMEM((2 * nz, nz), bf16),
            pltpu.VMEM((ny, 2 * ny), bf16),
            pltpu.VMEM((cx, ny, nz), f32),
            pltpu.VMEM((steps, groups, 128), f32),
            pltpu.VMEM((steps, n - 1, groups, 128), f32),
            pltpu.VMEM((groups, 128), f32),
            pltpu.SemaphoreType.DMA((2, 2)),
            pltpu.SemaphoreType.DMA((3, 2, 2)),
            pltpu.SemaphoreType.DMA((2, 2)),
            pltpu.SemaphoreType.DMA((3, 2, 2)),
            pltpu.SemaphoreType.DMA((steps,)),
            pltpu.SemaphoreType.DMA((steps,)),
            pltpu.SemaphoreType.DMA((2,)),
            pltpu.SemaphoreType.DMA((2,)),
        ],
        compiler_params=pltpu.CompilerParams(
            collective_id=0, has_side_effects=True, vmem_limit_bytes=56 * 2**20
        ),
        name="wave",
    )(
        c,
        wave_prev,
        wave_now,
        adj_late,
        adj_last,
        wavelet,
        source,
        row[None, :],
        z[None, :],
        row[:, None],
        z[:, None],
        observed.reshape(steps, groups, 128),
    )
    return grad, wide, resid.reshape(steps, nrec)


def prior_kernel(wide, grad, w1, w2, w3, b1, b2, b3, model_ref, planes, shifted, acc, bias1, bias2):
    cx, ny, nz = grad.shape
    deep = planes.shape[0] // ny
    span = 4
    planes[...] = jnp.zeros(planes.shape, jnp.float32)
    for x in range(cx + 4):
        planes[pl.ds(x, ny, stride=deep), :] = wide[x].astype(jnp.float32)
    shifted[0] = jnp.zeros(shifted.shape[1:], jnp.bfloat16)
    shifted[ny + 1] = jnp.zeros(shifted.shape[1:], jnp.bfloat16)
    acc[...] = jnp.zeros(acc.shape, jnp.float32)
    bias1[...] = jnp.broadcast_to(b1[...], bias1.shape)
    bias2[...] = jnp.broadcast_to(b2[...], bias2.shape)
    block = 8
    lane = lax.broadcasted_iota(jnp.int32, (block * deep, nz), 1)

    def shift(j, carry):
        v = planes[pl.ds(pl.multiple_of(j * block * deep, block * deep), block * deep), :]
        ahead = jnp.where(lane >= 1, pltpu.roll(v, 1, 1), 0.0)
        behind = jnp.where(lane < nz - 1, pltpu.roll(v, nz - 1, 1), 0.0)
        for c, part in enumerate((ahead, v, behind)):
            shifted[pl.ds(1 + j * block, block), c] = part.astype(jnp.bfloat16).reshape(
                block, deep, nz
            )
        return carry

    lax.fori_loop(0, ny // block, shift, 0)
    half = w2.shape[0]
    rest = w1.shape[0] - half
    small = lax.broadcasted_iota(jnp.int32, (cx, nz), 1)

    def rows(j, carry):
        y0 = j * span
        cells = jnp.concatenate(
            [shifted[pl.ds(y0 + k, 3)].reshape(9 * deep, nz) for k in range(span)], axis=1
        )
        lifted = jnp.dot(w1[...], cells, preferred_element_type=jnp.float32) + bias1[...]
        lifted = jnp.maximum(lifted, 0.0).astype(jnp.bfloat16)
        hidden = jnp.concatenate(
            [
                jnp.dot(w2[...], lifted[:half], preferred_element_type=jnp.float32),
                jnp.dot(w2[:rest, :rest], lifted[half:], preferred_element_type=jnp.float32),
            ],
            axis=0,
        )
        hidden = jnp.maximum(hidden + bias2[...], 0.0).astype(jnp.bfloat16)
        out = jnp.dot(w3[...], hidden, preferred_element_type=jnp.float32)
        for k in range(span):
            for b in range(3):
                c0, c1, c2 = [
                    out[(3 * b + c) * cx : (3 * b + c + 1) * cx, k * nz : (k + 1) * nz]
                    for c in range(3)
                ]
                total = c1 + jnp.where(small >= 1, pltpu.roll(c0, 1, 1), 0.0)
                total += jnp.where(small < nz - 1, pltpu.roll(c2, nz - 1, 1), 0.0)
                at = pl.ds(pl.multiple_of((y0 + k + 2 - b) * cx, cx), cx)
                acc[at, :] = acc[at, :] + total
        return carry

    lax.fori_loop(0, ny // span, rows, 0)
    for x in range(cx):
        conv = acc[pl.ds(cx + x, ny, stride=cx), :] + b3[0]
        model_ref[x] = (grad[x] + conv).astype(jnp.bfloat16)


def prior(wide, grad, weight_in, bias_in, weight_mix, bias_mix, weight_out, bias_out):
    cx, ny, nz = grad.shape
    ch = weight_in.shape[0]
    bf16, f32 = jnp.bfloat16, jnp.float32
    deep = 16
    held = cx + 2
    near = np.zeros((held, 3, deep), np.float32)
    far = np.zeros((cx, 3, held), np.float32)
    for a in range(3):
        for x in range(held):
            near[x, a, x + a] = 1.0
        for x in range(cx):
            far[x, a, x + a] = 1.0
    w1 = jnp.einsum("xai,hak->xhki", near.astype(bf16), weight_in.reshape(ch, 3, 9))
    w1 = w1.reshape(held * ch, 9 * deep)
    w2 = jnp.einsum("xi,hk->xhik", np.eye(cx, dtype=np.float32).astype(bf16), weight_mix)
    w2 = w2.reshape(cx * ch, cx * ch)
    margin = lax.axis_index("gx") * cx - 1 + jnp.arange(held, dtype=jnp.int32)
    keep = (margin >= 0) & (margin < cx * lax.axis_size("gx"))
    band = jnp.where(keep[None, None], far, 0.0).astype(bf16)
    w3 = jnp.einsum("xai,akh->kxih", band, weight_out.reshape(3, 9, ch))
    w3 = w3.reshape(9 * cx, held * ch)
    b1 = jnp.tile(bias_in, held)[:, None]
    b2 = jnp.tile(bias_mix, held)[:, None]
    vmem = pl.BlockSpec(memory_space=pltpu.VMEM)
    smem = pl.BlockSpec(memory_space=pltpu.SMEM)
    return pl.pallas_call(
        prior_kernel,
        out_shape=jax.ShapeDtypeStruct((cx, ny, nz), bf16),
        in_specs=[vmem] * 7 + [smem],
        out_specs=vmem,
        scratch_shapes=[
            pltpu.VMEM((ny * deep, nz), f32),
            pltpu.VMEM((ny + 2, 3, deep, nz), bf16),
            pltpu.VMEM(((ny + 2) * cx, nz), f32),
            pltpu.VMEM((held * ch, 4 * nz), f32),
            pltpu.VMEM((held * ch, 4 * nz), f32),
        ],
        compiler_params=pltpu.CompilerParams(vmem_limit_bytes=40 * 2**20),
        name="prior",
    )(wide, grad, w1.astype(bf16), w2.astype(bf16), w3.astype(bf16), b1, b2, bias_out)


def route_kernel(n, cap, model, owner_sub, owner_lane, print_lane, out, buckets, own, send, recv):
    cx, ny, nz = model.shape
    me = lax.axis_index("gx")
    shot = lax.axis_index("shots")
    barrier = pltpu.get_barrier_semaphore()

    def greet(d, carry):
        pl.semaphore_signal(
            barrier, inc=1, device_id=(shot, lax.rem(me + d, n)), device_id_type=MESH
        )
        return carry

    lax.fori_loop(1, n, greet, 0)
    before = lax.broadcasted_iota(jnp.int32, (ny, ny), 0)
    after = lax.broadcasted_iota(jnp.int32, (ny, ny), 1)
    same = jnp.where((owner_sub[...] == owner_lane[...]) & (before < after), 1.0, 0.0)
    slots = jnp.sum(same, axis=0, keepdims=True).astype(jnp.int32)
    place = owner_lane[...] * cap + slots
    place = jnp.where(print_lane[...] == 1, place, -1)
    at = lax.broadcasted_iota(jnp.int32, (n * cap, ny), 0)
    pick = jnp.where(at == place, 1.0, 0.0).astype(jnp.bfloat16)
    for x in range(cx):
        part = jnp.dot(pick, model[x], preferred_element_type=jnp.float32).astype(jnp.bfloat16)
        buckets[:, :, x * nz : (x + 1) * nz] = part.reshape(n, cap, nz)
    pl.semaphore_wait(barrier, n - 1)

    def copy(d):
        to = lax.rem(me + d, n)
        return pltpu.make_async_remote_copy(
            src_ref=buckets.at[to],
            dst_ref=out.at[me],
            send_sem=send.at[d],
            recv_sem=recv.at[d],
            device_id=(shot, to),
            device_id_type=MESH,
        )

    def landed(d):
        source = lax.rem(me - d + n, n)
        return pltpu.make_async_copy(out.at[source], out.at[source], recv.at[d])

    mine = pltpu.make_async_copy(buckets.at[me], out.at[me], own)

    def start(d, carry):
        copy(d).start()
        return carry

    def finish(d, carry):
        copy(d).wait_send()
        landed(d).wait()
        return carry

    lax.fori_loop(1, n, start, 0)
    mine.start()
    mine.wait()
    lax.fori_loop(1, n, finish, 0)


def route(n, cap, model, owner, footprint):
    cx, ny, nz = model.shape
    vmem = pl.BlockSpec(memory_space=pltpu.VMEM)
    return pl.pallas_call(
        functools.partial(route_kernel, n, cap),
        out_shape=jax.ShapeDtypeStruct((n, cap, cx * nz), jnp.bfloat16),
        in_specs=[vmem] * 4,
        out_specs=pl.BlockSpec(memory_space=pl.ANY),
        scratch_shapes=[
            pltpu.VMEM((n, cap, cx * nz), jnp.bfloat16),
            pltpu.SemaphoreType.DMA,
            pltpu.SemaphoreType.DMA((n,)),
            pltpu.SemaphoreType.DMA((n,)),
        ],
        compiler_params=pltpu.CompilerParams(
            collective_id=1, has_side_effects=True, vmem_limit_bytes=24 * 2**20
        ),
        name="route",
    )(model, owner, owner.reshape(1, ny), footprint.reshape(1, ny))


def per_device(
    courant_sq,
    wave_prev,
    wave_now,
    adj_late,
    adj_last,
    wavelet,
    source_cell,
    receivers,
    observed,
    footprint,
    brick_owner,
    prior_in,
    prior_in_bias,
    prior_mix,
    prior_mix_bias,
    prior_out,
    prior_out_bias,
):
    cells_x, cells_y, cells_z = wave_now.shape
    devices = lax.axis_size("gx")
    grad, grad_wide, residual_traces = wave(
        devices,
        courant_sq,
        wave_prev,
        wave_now,
        adj_late,
        adj_last,
        wavelet,
        source_cell,
        receivers,
        observed,
    )
    model_grad = prior(
        grad_wide,
        grad,
        prior_in,
        prior_in_bias,
        prior_mix,
        prior_mix_bias,
        prior_out,
        prior_out_bias,
    )
    capacity = max(2, 2 * cells_y // devices)
    if capacity % 16 == 0:
        arrived = route(devices, capacity, model_grad, brick_owner, footprint)
        return (residual_traces, arrived[None])
    bricks = model_grad.transpose(1, 0, 2).reshape(cells_y, cells_x * cells_z)
    bricks = jnp.where((footprint == 1)[:, None], bricks, jnp.zeros_like(bricks))
    owners = brick_owner[:, 0]
    same = owners[:, None] == owners[None, :]
    lower = (
        jnp.arange(cells_y, dtype=jnp.int32)[:, None]
        > jnp.arange(cells_y, dtype=jnp.int32)[None, :]
    )
    slots = jnp.sum((same & lower).astype(jnp.int32), axis=1)
    buckets = (
        jnp.zeros((devices, capacity, cells_x * cells_z), jnp.bfloat16)
        .at[owners, slots]
        .set(bricks)
    )
    arrived = lax.all_to_all(buckets, "gx", split_axis=0, concat_axis=0, tiled=True)
    return (residual_traces, arrived[None])


def solution(mesh):
    return jax.shard_map(
        per_device,
        mesh=mesh,
        in_specs=(
            P("gx", None, None),
            P(("shots", "gx"), None, None),
            P(("shots", "gx"), None, None),
            P(("shots", "gx"), None, None),
            P(("shots", "gx"), None, None),
            P("shots"),
            P("shots"),
            P("shots"),
            P("shots", None),
            P(("shots", "gx")),
            P("gx", None),
            P(),
            P(),
            P(),
            P(),
            P(),
            P(),
        ),
        out_specs=(P("shots", None), P(("shots", "gx"), None, None, None)),
        check_vma=False,
    )
```
